512 devices in a mesh: wide: 64 (over z, x, core), kv: 8 (over y).
Axes of the slice: x: 4, y: 8, z: 8, core: 2. Of those that a mesh axis runs over, the one named last changes fastest.
Arguments:
- queries: bfloat16 [256, 2, 8192], P('wide', None, 'kv'), may hold values from -14 to 14
- new_kv: bfloat16 [256, 2, 8, 256], P('wide', None, 'kv'), may hold values from -6 to 6
- suffix_cache: bfloat16 [256, 512, 8, 256], P('wide', None, 'kv'), may hold values from -14 to 14
- suffix_len: int32 [256], P('wide'), may hold values from 1 to 512, 98304 in all
- prefix_cache: bfloat16 [32768, 8, 256], P('wide', 'kv'), may hold values from -14 to 14
- prompt_len: int32 [8], replicated, may hold values from 1 to 4096, 16384 in all
- prompt_slot: int32 [8], replicated, may hold values from 0 to 7, each once
- sample_prompt: int32 [256, 1], replicated, may hold values from 0 to 7; in each aligned block of 4 rows (0 to 3, 4 to 7, ...) at most 2 rows name the same one
- out_weight: bfloat16 [8192, 8192], P('kv', 'wide'), may hold values from -0.0625 to 0.0625
Outputs:
- mixed: bfloat16 [256, 2, 8192], P('kv', None, 'wide')
The draws below stay inside these ranges and needn't reach their ends.
Inputs may be any that keep to these rules, and one draw needn't show every extreme that they name: A permutation: prompt p's cache occupies rows prompt_slot[p] * 4096 to prompt_slot[p] * 4096 + 4095 of prefix_cache. `sample_prompt`: sample i is held by wide index i // 4; among the samples of one wide index at most 2 continue the same prompt.
All inputs are finite; a program needn't handle non-finite values. No bound on the sum of `suffix_len` on one device may be relied on, other than what follows from the above.
Results may differ from the reference program's by a relative error of at most 0.0061.
Values may be sent and summed in bfloat16 or wider, within the bound.
No kernel may reach another device: no remote copies, remote signals or barrier semaphores. Data moves between devices by JAX's collectives and lax.ppermute only.
A program may use at most 64 MiB of HBM per device.

```python
import math
import jax
import jax.numpy as jnp
import numpy as np
from jax import lax

D = 8192
HQ = 64
KVH = 8
HD = 128
GROUP = 8
STEPS = 2
PSH = 512
SUF = 512
SAMP_DEV = 4
NPROMPT = 8
MOST = 2
PLEN = 4096
NSAMP = 256
N_WIDE = 64


def draw_queries(key, part):
    key = jax.random.fold_in(key, 11)
    key_one = jax.random.fold_in(key, 0)
    full_shape = (NSAMP, STEPS, HQ * HD)
    values = jnp.clip(2.0 * jax.random.normal(key_one, full_shape, jnp.float32), -8.0, 8.0)
    return values.astype(jnp.bfloat16)


def cache_rows(key, blocks, block_len):
    key_one, key_two = jax.random.split(key, 2)
    key_part = jnp.clip(jax.random.normal(key_one, (blocks, block_len, KVH, HD), jnp.float32), -6.0, 6.0)
    value_part = jnp.clip(2.0 * jax.random.normal(key_two, (blocks, block_len, KVH, HD), jnp.float32), -8.0, 8.0)
    return jnp.concatenate([key_part, value_part], axis=-1)


def draw_prefix_cache(key, part):
    key = jax.random.fold_in(key, 23)
    rows = cache_rows(key, NPROMPT * PLEN // PSH, PSH)
    return rows.reshape(NPROMPT * PLEN, KVH, 2 * HD).astype(jnp.bfloat16)


def draw_suffix_cache(key, part):
    key = jax.random.fold_in(key, 37)
    rows = cache_rows(key, NSAMP, SUF)
    return rows.astype(jnp.bfloat16)


def level_of(own_key, extent, shards, low, high):
    loudness = 1.0
    for dim, blocks in shards:
        heights = jax.random.uniform(jax.random.fold_in(jax.random.fold_in(own_key, 6), dim), (blocks,), jnp.float32, low / len(shards), high / len(shards))
        loudness = loudness * jnp.repeat(jnp.exp(heights), extent[dim] // blocks).reshape((-1,) + (1,) * (len(extent) - 1 - dim))
    return loudness


def profile(number_of, total, limit, slope):
    weights = [(1 << 20) // math.isqrt(standing ** slope) + 1 for standing in range(2, number_of + 1)]
    rest, holding = total - limit - (number_of - 1), [1] * (number_of - 1)
    while rest > 0:
        candidates = [i for i in range(number_of - 1) if holding[i] < limit]
        mass, left = sum([weights[i] for i in candidates]), rest
        for i in candidates:
            more = min(limit - holding[i], max(1, left * weights[i] // mass), rest)
            holding[i] = holding[i] + more
            rest = rest - more
    return np.array([limit] + holding)


def uneven(stream_key, amount, total, most, skew):
    if amount == 2:
        one = jax.random.randint(stream_key, (), max(1, total - most), min(most, total - 1) + 1)
        return jnp.stack([one, total - one])
    lengths = jnp.asarray(profile(amount, total, most, skew), jnp.int32)
    couples = (amount - 1) // 2
    donor, receiver = lengths[1:1 + 2 * couples:2], lengths[2:2 + 2 * couples:2]
    room = jnp.minimum(donor - 1, most - receiver)
    shifted = jax.random.randint(jax.random.fold_in(stream_key, 1), (couples,), 0, 1 << 20) % (room + 1)
    lengths = lengths.at[1:1 + 2 * couples:2].set(donor - shifted).at[2:2 + 2 * couples:2].set(receiver + shifted)
    return lengths[jax.random.permutation(jax.random.fold_in(stream_key, 2), amount)]


def deal_out(stream_key, own, number, rows, count, top, reach, skew):
    order = jax.random.permutation(stream_key, count)
    heavy_load, usual = shares(count, rows * top, reach, skew, True), shares(count, rows * top, reach, skew, False)
    places = jnp.arange(count)

    def named(tallies, turn):
        used = int((tallies > 0).sum())
        fixed = max(1, used // 4)
        moved = fixed + (places - fixed + turn * (used - fixed)) % max(1, count - fixed)
        return jnp.zeros((count,), jnp.int32).at[order[jnp.where(places < fixed, places, moved)]].set(jnp.asarray(tallies, jnp.int32))

    tallies = jnp.where(number % 4 == 0, named(heavy_load, number // 4), named(usual, number - number // 4 - 1))
    mixed = jax.random.permutation(jax.random.fold_in(own, 3), count)
    source_of, taker = mixed[0:count // 2 * 2:2], mixed[1:count // 2 * 2:2]
    slack = jnp.minimum(tallies[source_of] - 1, reach - tallies[taker]) // 2
    slack = jnp.where((source_of == order[0]) | (taker == order[0]) | (tallies[taker] == 0), 0, jnp.maximum(slack, 0))
    moved = jax.random.randint(jax.random.fold_in(own, 4), (count // 2,), 0, 1 << 20) % (slack + 1)
    tallies = tallies.at[source_of].add(-moved).at[taker].add(moved)
    items = jnp.searchsorted(jnp.cumsum(tallies), jnp.arange(rows * top), side="right").astype(jnp.int32)
    table = items.reshape(top, rows).T
    table = table[jax.random.permutation(jax.random.fold_in(own, 1), rows)]
    turn = jax.random.randint(jax.random.fold_in(own, 2), (rows, 1), 0, top)
    return jnp.take_along_axis(table, (jnp.arange(top)[None, :] + turn) % top, axis=1)


def shares(amount, total, limit, lean, full):
    loads = [(1 << 20) // math.isqrt(rank ** lean) + 1 for rank in range(1, amount + 1)]
    largest = limit if full else min(limit, max(-(-total // amount), total * loads[0] // sum(loads)))
    least = 1 if total - largest >= amount - 1 else 0
    given, rest = [largest] + [least] * (amount - 1), total - largest - least * (amount - 1)
    while rest > 0:
        candidates = [i for i in range(1, amount) if given[i] < largest] or [i for i in range(1, amount) if given[i] < limit]
        whole, remaining = sum([loads[i] for i in candidates]), rest
        for i in candidates:
            extra = min(limit - given[i], max(1, remaining * loads[i] // whole), rest)
            given[i] = given[i] + extra
            rest = rest - extra
    return np.array(given)


def bell_draw(own_key, dims, spread, most, cuts=(), kind=jnp.bfloat16):
    values = spread * jax.random.normal(own_key, dims, jnp.float32)
    if cuts:
        values = values * level_of(own_key, dims, cuts, -0.22, 0.18)
    return jnp.clip(values, -most, most).astype(kind)


def setup_inputs(seed: int = 0) -> dict:
    key_list = jax.random.split(jax.random.key(seed), 10)
    queries = draw_queries(jax.random.fold_in(key_list[9], 71), 0)
    new_kv = bell_draw(key_list[1], (NSAMP, STEPS, KVH, 2 * HD), 1.5, 6.0, ((0, 64), (2, 8)))
    suffix_cache = draw_suffix_cache(jax.random.fold_in(key_list[9], 71), 0)
    suffix_len = uneven(key_list[3], NSAMP, NSAMP * SUF * 3 // 4, SUF, 1).astype(jnp.int32)
    prefix_cache = draw_prefix_cache(jax.random.fold_in(key_list[9], 71), 0)
    prompt_len = uneven(key_list[5], NPROMPT, NPROMPT * PLEN // 2, PLEN, 2).astype(jnp.int32)
    prompt_slot = jax.random.permutation(key_list[6], NPROMPT).astype(jnp.int32)
    sample_prompt_keys = jax.random.split(jax.random.fold_in(key_list[7], 1), NSAMP // SAMP_DEV)
    sample_prompt_turns = jax.random.permutation(jax.random.fold_in(key_list[7], 3), NSAMP // SAMP_DEV)
    sample_prompt = jax.vmap(lambda own, number: deal_out(jax.random.fold_in(key_list[7], 2), own, number, SAMP_DEV, NPROMPT, 1, MOST, 2))(sample_prompt_keys, sample_prompt_turns).reshape((NSAMP, 1))
    out_weight = bell_draw(key_list[8], (HQ * HD, D), (HQ * HD) ** -0.5, 0.0625, ((0, 8), (1, 64)))
    return {"queries": queries, "new_kv": new_kv, "suffix_cache": suffix_cache, "suffix_len": suffix_len, "prefix_cache": prefix_cache, "prompt_len": prompt_len, "prompt_slot": prompt_slot, "sample_prompt": sample_prompt, "out_weight": out_weight}


def reference(queries, new_kv, suffix_cache, suffix_len, prefix_cache, prompt_len, prompt_slot, sample_prompt, out_weight):
    split_count = N_WIDE // NPROMPT
    scale = HD ** -0.5

    def one_sample(sample_index):
        prompt = sample_prompt[sample_index, 0]
        first_row = (prompt_slot[prompt] * PLEN).astype(jnp.int32)
        prompt_cache = lax.dynamic_slice_in_dim(prefix_cache, first_row, PLEN, 0).astype(jnp.float32)
        query_rows = queries[sample_index].astype(jnp.float32).reshape(STEPS, KVH, GROUP, HD)
        scores = jnp.einsum("tgxd,jgd->tgxj", query_rows, prompt_cache[:, :, :HD]) * scale
        scores = scores.reshape(STEPS, KVH, GROUP, split_count, PSH)
        usable = (jnp.arange(PLEN) < prompt_len[prompt]).reshape(split_count, PSH)
        masked = jnp.where(usable, scores, -1e30)
        seg_max = jnp.max(masked, axis=-1)
        weights = jnp.where(usable, jnp.exp(masked - seg_max[..., None]), 0.0)
        seg_sum = jnp.sum(weights, axis=-1)
        seg_probs = lax.optimization_barrier((weights / jnp.maximum(seg_sum, 1.0)[..., None]).astype(jnp.bfloat16))
        prompt_values = prompt_cache[:, :, HD:].reshape(split_count, PSH, KVH, HD)
        seg_out = jnp.einsum("tgxsj,sjgd->tgxsd", seg_probs.astype(jnp.float32), prompt_values)
        seg_out = lax.optimization_barrier(seg_out.astype(jnp.bfloat16)).astype(jnp.float32)

        local_rows = jnp.concatenate([suffix_cache[sample_index], new_kv[sample_index]], axis=0).astype(jnp.float32)
        local_scores = jnp.einsum("tgxd,jgd->tgxj", query_rows, local_rows[:, :, :HD]) * scale
        positions = jnp.arange(SUF + STEPS)
        step_ids = jnp.arange(STEPS)
        local_ok = jnp.where(positions[None, :] < SUF, positions[None, :] < suffix_len[sample_index], positions[None, :] - SUF <= step_ids[:, None])
        local_ok = local_ok[:, None, None, :]
        local_masked = jnp.where(local_ok, local_scores, -1e30)
        local_max = jnp.max(local_masked, axis=-1)
        local_weights = jnp.where(local_ok, jnp.exp(local_masked - local_max[..., None]), 0.0)
        local_sum = jnp.sum(local_weights, axis=-1)
        local_probs = lax.optimization_barrier((local_weights / local_sum[..., None]).astype(jnp.bfloat16))
        local_out = jnp.einsum("tgxj,jgd->tgxd", local_probs.astype(jnp.float32), local_rows[:, :, HD:])

        overall = jnp.maximum(jnp.max(seg_max, axis=-1), local_max)
        seg_weight = seg_sum * jnp.exp(seg_max - overall[..., None])
        local_weight = local_sum * jnp.exp(local_max - overall)
        numerator = jnp.sum(seg_weight[..., None] * seg_out, axis=3) + local_weight[..., None] * local_out
        denominator = jnp.sum(seg_weight, axis=-1) + local_weight
        attn = (numerator / denominator[..., None]).astype(jnp.bfloat16)
        return attn.reshape(STEPS, HQ * HD)

    attn_all = lax.map(one_sample, jnp.arange(NSAMP))
    mixed = jnp.dot(attn_all.reshape(NSAMP * STEPS, HQ * HD), out_weight, preferred_element_type=jnp.float32)
    return mixed.astype(jnp.bfloat16).reshape(NSAMP, STEPS, D)
```

```python
import jax
import jax.numpy as jnp
from jax import lax
from jax.sharding import PartitionSpec as P

HD = 128
GROUP = 8
STEPS = 2
PSH = 512
NPROMPT = 8
MOST = 2
CORES = 2
QROWS = STEPS * GROUP
LSE_ROWS = 8
NEG = -1e30
F32 = jnp.float32
BF16 = jnp.bfloat16


def sample_ranks(prompts):
    length = prompts.shape[0]
    earlier = jnp.arange(length)[None, :] < jnp.arange(length)[:, None]
    return jnp.sum((prompts[:, None] == prompts[None, :]) & earlier, axis=-1)


def split3(x):
    hi = lax.reduce_precision(x, 8, 7)
    mid = lax.reduce_precision(x - hi, 8, 7)
    low = x - hi - mid
    return hi.astype(BF16), mid.astype(BF16), low.astype(BF16)


def per_device(
    queries, new_kv, suffix_cache, suffix_len, prefix_cache, prompt_len, prompt_slot, sample_prompt, out_weight
):
    wide = lax.axis_size("wide")
    kvs = lax.axis_size("kv")
    held = queries.shape[0]
    ring = wide // NPROMPT
    chips = ring // CORES
    position = lax.axis_index("wide")
    scale = HD ** (-0.5)

    same_core = [[p * CORES + c for p in range(wide // CORES)] for c in range(CORES)]
    planes = [[z * ring + i for i in range(ring)] for z in range(NPROMPT)]
    columns = [[z * ring + i for z in range(NPROMPT)] for i in range(ring)]
    swap = [(i, i ^ 1) for i in range(wide)]

    weights = lax.all_gather(out_weight, "wide", axis=0, tiled=False, axis_index_groups=columns)

    own_cache = prefix_cache[:, 0, :]
    other_cache = lax.ppermute(own_cache, "wide", swap)

    my_prompts = lax.dynamic_slice_in_dim(sample_prompt[:, 0], position * held, held)
    prompt_range = jnp.arange(NPROMPT)
    my_group = jnp.sum(
        jnp.where(my_prompts[:, None] == prompt_range[None, :], prompt_slot[None, :], 0), axis=1
    )
    my_rank = sample_ranks(my_prompts)
    picked = (my_group[:, None, None] == prompt_range[None, :, None]) & (
        my_rank[:, None, None] == jnp.arange(MOST)[None, None, :]
    )
    rows = queries.reshape(held, QROWS, HD)
    sent = jnp.zeros((NPROMPT, chips, MOST, QROWS, HD), BF16)
    for r in range(held):
        sent = jnp.where(picked[r][:, None, :, None, None], rows[r][None, None, None], sent)
    sent = sent.reshape(NPROMPT * chips, MOST * QROWS, HD)
    asked = lax.all_to_all(sent, "wide", 0, 0, tiled=True, axis_index_groups=same_core)

    owner = prompt_slot == position // ring
    prompt_rows = jnp.sum(jnp.where(owner, prompt_len, 0))
    segment = position % ring
    count = asked.shape[0] * asked.shape[1]
    flat = asked.reshape(count, HD)
    j = jnp.arange(PSH)
    ok_own = (segment * PSH + j < prompt_rows)[None, :]
    ok_other = ((segment ^ 1) * PSH + j < prompt_rows)[None, :]

    def scores(cache, ok):
        s = jnp.einsum("nd,jd->nj", flat, cache[:, :HD], preferred_element_type=F32) * scale
        return jnp.where(ok, s, NEG)

    s_own, s_other = scores(own_cache, ok_own), scores(other_cache, ok_other)
    top = jnp.maximum(jnp.max(s_own, axis=1), jnp.max(s_other, axis=1))
    e_own = jnp.where(ok_own, jnp.exp(s_own - top[:, None]), 0.0)
    e_other = jnp.where(ok_other, jnp.exp(s_other - top[:, None]), 0.0)
    total = jnp.sum(e_own, axis=1) + jnp.sum(e_other, axis=1)
    part = jnp.einsum(
        "nj,jd->nd", e_own.astype(BF16), own_cache[:, HD:], preferred_element_type=F32
    ) + jnp.einsum(
        "nj,jd->nd", e_other.astype(BF16), other_cache[:, HD:], preferred_element_type=F32
    )
    safe = jnp.maximum(total, 1.0)
    part = (part / safe[:, None]).astype(BF16).reshape(asked.shape)
    lse = jnp.where(total > 0, top + jnp.log(safe), NEG).reshape(asked.shape[:2])
    pieces = jnp.stack(split3(lse), axis=1)
    pieces = jnp.pad(pieces, ((0, 0), (0, LSE_ROWS - 3), (0, HD - MOST * QROWS)))
    reply = jnp.concatenate([part, pieces], axis=1)
    back = lax.all_to_all(reply, "wide", 0, 0, tiled=True, axis_index_groups=same_core)

    suffix_keys = suffix_cache[:, :, 0, :HD]
    suffix_vals = suffix_cache[:, :, 0, HD:]
    new_keys = new_kv[:, :, 0, :HD]
    new_vals = new_kv[:, :, 0, HD:]
    s_old = jnp.einsum("rhd,rjd->rhj", rows, suffix_keys, preferred_element_type=F32) * scale
    s_new = jnp.einsum("rhd,rud->rhu", rows, new_keys, preferred_element_type=F32) * scale
    ok_old = (jnp.arange(suffix_cache.shape[1])[None, :] < suffix_len[:, None])[:, None, :]
    ok_new = (jnp.arange(STEPS)[None, :] <= jnp.arange(QROWS)[:, None] // GROUP)[None]
    s_old = jnp.where(ok_old, s_old, NEG)
    s_new = jnp.where(ok_new, s_new, NEG)
    local_max = jnp.maximum(jnp.max(s_old, axis=-1), jnp.max(s_new, axis=-1))
    e_old = jnp.where(ok_old, jnp.exp(s_old - local_max[..., None]), 0.0)
    e_new = jnp.where(ok_new, jnp.exp(s_new - local_max[..., None]), 0.0)
    local_sum = jnp.sum(e_old, axis=-1) + jnp.sum(e_new, axis=-1)
    local_out = jnp.einsum(
        "rhj,rjd->rhd", e_old.astype(BF16), suffix_vals, preferred_element_type=F32
    ) + jnp.einsum("rhu,rud->rhd", e_new.astype(BF16), new_vals, preferred_element_type=F32)

    back = back.reshape(NPROMPT, chips, MOST * QROWS + LSE_ROWS, HD)
    outs = back[:, :, : MOST * QROWS].reshape(NPROMPT, chips, MOST, QROWS, HD)
    lses = back[:, :, MOST * QROWS : MOST * QROWS + 3, : MOST * QROWS].astype(F32)
    lses = (lses[:, :, 0] + lses[:, :, 1]) + lses[:, :, 2]
    lses = lses.reshape(NPROMPT, chips, MOST, QROWS)
    pick_bf = picked.astype(BF16)
    prefix_out = jnp.einsum("rgc,gxchd->rxhd", pick_bf, outs, preferred_element_type=F32)
    prefix_lse = jnp.sum(
        jnp.where(picked[:, :, None, :, None], lses[None], 0.0), axis=(1, 3)
    )
    overall = jnp.maximum(jnp.max(prefix_lse, axis=1), local_max)
    seg_weight = jnp.exp(prefix_lse - overall[:, None])
    local_weight = jnp.exp(local_max - overall)
    numerator = (
        jnp.sum(seg_weight[..., None] * prefix_out, axis=1) + local_weight[..., None] * local_out
    )
    denominator = jnp.sum(seg_weight, axis=1) + local_weight * local_sum
    attn = (numerator / denominator[..., None]).astype(BF16).reshape(held * STEPS, GROUP * HD)

    spread = jnp.broadcast_to(attn[None], (ring,) + attn.shape)
    plane = lax.all_to_all(spread, "wide", 0, 0, tiled=True, axis_index_groups=planes)
    plane = plane.reshape(ring * held * STEPS, GROUP * HD)
    terms = jnp.einsum("nk,zkd->znd", plane, weights, preferred_element_type=F32).astype(BF16)
    terms = lax.all_to_all(terms, "kv", 0, 0, tiled=True)
    mine = jnp.sum(terms.astype(F32), axis=0).astype(BF16)
    turn = [
        ((z * ring + i) * kvs + y, (y * ring + i) * kvs + z)
        for z in range(NPROMPT)
        for i in range(ring)
        for y in range(kvs)
    ]
    mine = lax.ppermute(mine, ("wide", "kv"), turn)
    return mine.reshape(ring * held, STEPS, HD)


def solution(mesh):
    return jax.shard_map(
        per_device,
        mesh=mesh,
        in_specs=(
            P("wide", None, "kv"),
            P("wide", None, "kv", None),
            P("wide", None, "kv", None),
            P("wide"),
            P("wide", "kv", None),
            P(),
            P(),
            P(),
            P("kv", "wide"),
        ),
        out_specs=P("kv", None, "wide"),
        check_vma=False,
    )
```

```python
import jax
import jax.numpy as jnp
from jax import lax
from jax.sharding import PartitionSpec as P

HD = 128
GROUP = 8
STEPS = 2
PSH = 512
NPROMPT = 8
MOST = 2
CORES = 2
QROWS = STEPS * GROUP
LSE_ROWS = 8
NEG = -1e30
F32 = jnp.float32
BF16 = jnp.bfloat16


def sample_ranks(prompts):
    length = prompts.shape[0]
    earlier = jnp.arange(length)[None, :] < jnp.arange(length)[:, None]
    return jnp.sum((prompts[:, None] == prompts[None, :]) & earlier, axis=-1)


def split3(x):
    hi = lax.reduce_precision(x, 8, 7)
    mid = lax.reduce_precision(x - hi, 8, 7)
    low = x - hi - mid
    return hi.astype(BF16), mid.astype(BF16), low.astype(BF16)


def per_device(
    queries, new_kv, suffix_cache, suffix_len, prefix_cache, prompt_len, prompt_slot, sample_prompt, out_weight
):
    wide = lax.axis_size("wide")
    kvs = lax.axis_size("kv")
    held = queries.shape[0]
    ring = wide // NPROMPT
    chips = ring // CORES
    position = lax.axis_index("wide")
    scale = HD ** (-0.5)

    def index(z, x, c):
        return (z * chips + x) * CORES + c

    planes, cores = range(NPROMPT), range(CORES)
    along_x = [[index(z, x, c) for x in range(chips)] for z in planes for c in cores]
    same_x = [[index(z, x, c) for z in planes for c in cores] for x in range(chips)]
    along_xy = [
        [index(z, x, c) * kvs + y for x in range(chips) for y in range(kvs)]
        for z in planes
        for c in cores
    ]
    peers = NPROMPT * CORES

    def gather(block, groups):
        copies = jnp.broadcast_to(block[None], (len(groups[0]),) + block.shape)
        return lax.all_to_all(copies, "wide", 0, 0, tiled=True, axis_index_groups=groups)

    cache = gather(prefix_cache[:, 0, :], along_x)

    my_prompts = lax.dynamic_slice_in_dim(sample_prompt[:, 0], position * held, held)
    prompt_range = jnp.arange(NPROMPT)
    my_group = jnp.sum(
        jnp.where(my_prompts[:, None] == prompt_range[None, :], prompt_slot[None, :], 0), axis=1
    )
    my_rank = sample_ranks(my_prompts)
    picked = (my_group[:, None, None] == prompt_range[None, :, None]) & (
        my_rank[:, None, None] == jnp.arange(MOST)[None, None, :]
    )
    rows = queries.reshape(held, QROWS, HD)
    sent = jnp.zeros((NPROMPT, CORES, MOST, QROWS, HD), BF16)
    for r in range(held):
        sent = jnp.where(picked[r][:, None, :, None, None], rows[r][None, None, None], sent)
    sent = sent.reshape(peers, MOST * QROWS, HD)
    asked = lax.all_to_all(sent, "wide", 0, 0, tiled=True, axis_index_groups=same_x)

    owner = prompt_slot == position // ring
    prompt_rows = jnp.sum(jnp.where(owner, prompt_len, 0))
    core = position % CORES
    flat = asked.reshape(peers * MOST * QROWS, HD)
    segment = jnp.arange(chips) * CORES + core
    usable = (segment[:, None] * PSH + jnp.arange(PSH)[None, :] < prompt_rows)[None]
    s = jnp.einsum("nd,xjd->nxj", flat, cache[:, :, :HD], preferred_element_type=F32) * scale
    s = jnp.where(usable, s, NEG)
    top = jnp.max(s, axis=(1, 2))
    e = jnp.where(usable, jnp.exp(s - top[:, None, None]), 0.0)
    total = jnp.sum(e, axis=(1, 2))
    part = jnp.einsum("nxj,xjd->nd", e.astype(BF16), cache[:, :, HD:], preferred_element_type=F32)
    safe = jnp.maximum(total, 1.0)
    part = (part / safe[:, None]).astype(BF16).reshape(asked.shape)
    lse = jnp.where(total > 0, top + jnp.log(safe), NEG).reshape(asked.shape[:2])
    pieces = jnp.stack(split3(lse), axis=1)
    pieces = jnp.pad(pieces, ((0, 0), (0, LSE_ROWS - 3), (0, HD - MOST * QROWS)))
    reply = jnp.concatenate([part, pieces], axis=1)
    out_weight, reply = lax.optimization_barrier((out_weight, reply))
    back = lax.all_to_all(reply, "wide", 0, 0, tiled=True, axis_index_groups=same_x)

    weights = gather(out_weight, along_x)

    suffix_keys = suffix_cache[:, :, 0, :HD]
    suffix_vals = suffix_cache[:, :, 0, HD:]
    new_keys = new_kv[:, :, 0, :HD]
    new_vals = new_kv[:, :, 0, HD:]
    s_old = jnp.einsum("rhd,rjd->rhj", rows, suffix_keys, preferred_element_type=F32) * scale
    s_new = jnp.einsum("rhd,rud->rhu", rows, new_keys, preferred_element_type=F32) * scale
    ok_old = (jnp.arange(suffix_cache.shape[1])[None, :] < suffix_len[:, None])[:, None, :]
    ok_new = (jnp.arange(STEPS)[None, :] <= jnp.arange(QROWS)[:, None] // GROUP)[None]
    s_old = jnp.where(ok_old, s_old, NEG)
    s_new = jnp.where(ok_new, s_new, NEG)
    local_max = jnp.maximum(jnp.max(s_old, axis=-1), jnp.max(s_new, axis=-1))
    e_old = jnp.where(ok_old, jnp.exp(s_old - local_max[..., None]), 0.0)
    e_new = jnp.where(ok_new, jnp.exp(s_new - local_max[..., None]), 0.0)
    local_sum = jnp.sum(e_old, axis=-1) + jnp.sum(e_new, axis=-1)
    local_out = jnp.einsum(
        "rhj,rjd->rhd", e_old.astype(BF16), suffix_vals, preferred_element_type=F32
    ) + jnp.einsum("rhu,rud->rhd", e_new.astype(BF16), new_vals, preferred_element_type=F32)

    back = back.reshape(NPROMPT, CORES, MOST * QROWS + LSE_ROWS, HD)
    outs = back[:, :, : MOST * QROWS].reshape(NPROMPT, CORES, MOST, QROWS, HD)
    lses = back[:, :, MOST * QROWS : MOST * QROWS + 3, : MOST * QROWS].astype(F32)
    lses = (lses[:, :, 0] + lses[:, :, 1]) + lses[:, :, 2]
    lses = lses.reshape(NPROMPT, CORES, MOST, QROWS)
    pick_bf = picked.astype(BF16)
    prefix_out = jnp.einsum("rgc,gxchd->rxhd", pick_bf, outs, preferred_element_type=F32)
    prefix_lse = jnp.sum(
        jnp.where(picked[:, :, None, :, None], lses[None], 0.0), axis=(1, 3)
    )
    overall = jnp.maximum(jnp.max(prefix_lse, axis=1), local_max)
    seg_weight = jnp.exp(prefix_lse - overall[:, None])
    local_weight = jnp.exp(local_max - overall)
    numerator = (
        jnp.sum(seg_weight[..., None] * prefix_out, axis=1) + local_weight[..., None] * local_out
    )
    denominator = jnp.sum(seg_weight, axis=1) + local_weight * local_sum
    attn = (numerator / denominator[..., None]).astype(BF16).reshape(held * STEPS, GROUP * HD)

    rows_in = gather(attn, same_x).reshape(peers * held * STEPS, GROUP * HD)
    terms = jnp.einsum("nk,xkd->xnd", rows_in, weights, preferred_element_type=F32).astype(BF16)
    terms = terms.reshape(chips * NPROMPT, CORES * held * STEPS, HD)
    terms = lax.all_to_all(terms, ("wide", "kv"), 0, 0, tiled=True, axis_index_groups=along_xy)
    terms = terms.reshape(chips, kvs, CORES * held * STEPS, HD)
    mine = jnp.sum(terms.astype(F32), axis=1).astype(BF16)
    return mine.reshape(ring * held, STEPS, HD)


def solution(mesh):
    return jax.shard_map(
        per_device,
        mesh=mesh,
        in_specs=(
            P("wide", None, "kv"),
            P("wide", None, "kv", None),
            P("wide", None, "kv", None),
            P("wide"),
            P("wide", "kv", None),
            P(),
            P(),
            P(),
            P("kv", "wide"),
        ),
        out_specs=P("kv", None, "wide"),
        check_vma=False,
    )
```

```python
import functools
import math

import jax
import jax.numpy as jnp
from jax import lax
from jax.experimental import pallas as pl
from jax.experimental.pallas import tpu as pltpu
from jax.sharding import PartitionSpec as P

HD = 128
GROUP = 8
STEPS = 2
PSH = 512
NPROMPT = 8
MOST = 2
CORES = 2
QROWS = STEPS * GROUP
LSE_ROWS = 8
CHUNK = 4
NEG = -1e30
SCALE = HD ** (-0.5)
LOG2E = 1.0 / math.log(2.0)
F32 = jnp.float32
BF16 = jnp.bfloat16
VMEM = pl.BlockSpec(memory_space=pltpu.VMEM)
SMEM = pl.BlockSpec(memory_space=pltpu.SMEM)


def shape(*dims, dtype=BF16):
    return jax.ShapeDtypeStruct(dims, dtype)


def call(kernel, name, out_shape, scalars, arrays, flops=0, exps=0):
    outs = list(out_shape)
    moved = sum(math.prod(a.shape) * a.dtype.itemsize for a in list(arrays) + outs)
    return pl.pallas_call(
        kernel,
        out_shape=outs,
        in_specs=[SMEM] * len(scalars) + [VMEM] * len(arrays),
        out_specs=[VMEM] * len(outs),
        compiler_params=pltpu.CompilerParams(vmem_limit_bytes=24 * 1024 * 1024),
        cost_estimate=pl.CostEstimate(flops=flops, bytes_accessed=moved, transcendentals=exps),
        name=name,
    )(*scalars, *arrays)


def places(first, prompts, slots, held):
    mine = [prompts[first + r] for r in range(held)]
    ranks = [
        sum(((mine[e] == mine[r]).astype(jnp.int32) for e in range(r)), jnp.int32(0)) for r in range(held)
    ]
    return [(slots[mine[r]], ranks[r]) for r in range(held)]


def asking_kernel(copies, where, prompts, slots, queries, cache, sent, rows, cache_out):
    held = queries.shape[0]
    cache_out[...] = cache[...]
    sent[...] = jnp.zeros_like(sent)
    for r, (slot, rank) in enumerate(places(where[0] * held, prompts, slots, held)):
        q = queries[r].astype(F32)
        q = jnp.concatenate([q[:, h * HD : (h + 1) * HD] for h in range(GROUP)], axis=0).astype(BF16)
        rows[r] = q
        for i in range(copies):
            sent[slot * copies + i, pl.ds(pl.multiple_of(rank * QROWS, QROWS), QROWS), :] = q


def split3(x):
    hi = x.astype(BF16).astype(F32)
    mid = (x - hi).astype(BF16).astype(F32)
    return hi, mid, x - hi - mid


def prefix_kernel(segments, where, slots, lens, asked, *refs):
    blocks, weight, reply, weight_out = refs[:-3], *refs[-3:]
    weight_out[...] = weight[...]
    length = jnp.int32(0)
    for p in range(NPROMPT):
        length = jnp.where(slots[p] == where[1], lens[p], length)
    per_source = MOST * QROWS
    some = CHUNK * per_source
    for first in range(0, asked.shape[0], CHUNK):
        rows = asked[first : first + CHUNK].reshape(some, HD)
        scores = []
        for k, block in enumerate(blocks):
            s = lax.dot_general(
                rows, block[:, :HD], (((1,), (1,)), ((), ())), preferred_element_type=F32
            )
            j = lax.broadcasted_iota(jnp.int32, (1, PSH), 1)
            scores.append(jnp.where(j < length - where[2 + k] * PSH, s, NEG))
        top = functools.reduce(jnp.maximum, [jnp.max(s, axis=1, keepdims=True) for s in scores])
        floor = jnp.maximum(top, 0.1 * NEG) * (SCALE * LOG2E)
        total, part = 0.0, 0.0
        for s, block in zip(scores, blocks):
            e = jnp.exp2(s * (SCALE * LOG2E) - floor)
            total += jnp.sum(e, axis=1, keepdims=True)
            part += jnp.dot(e.astype(BF16), block[:, HD:], preferred_element_type=F32)
        safe = jnp.maximum(total, 1.0)
        part = part / safe
        lse = jnp.where(total > 0.0, top * SCALE + jnp.log(safe), NEG)
        row = lax.broadcasted_iota(jnp.int32, (some, HD), 0)
        lane = lax.broadcasted_iota(jnp.int32, (some, HD), 1)
        lse = jnp.where(row % per_source == lane, lse, 0.0).reshape(CHUNK, per_source, HD)
        lse = jnp.sum(lse, axis=1, keepdims=True)
        hi, mid, low = split3(lse)
        at = lax.broadcasted_iota(jnp.int32, (CHUNK, LSE_ROWS, HD), 1)
        pieces = jnp.where(at == 0, hi, jnp.where(at == 1, mid, jnp.where(at == 2, low, 0.0)))
        reply[first : first + CHUNK] = jnp.concatenate(
            [part.reshape(CHUNK, per_source, HD).astype(BF16), pieces.astype(BF16)], axis=1
        )


def local_kernel(lens, rows, suffix, fresh, out, lse):
    for r in range(rows.shape[0]):
        q = rows[r]
        s = lax.dot_general(
            q, suffix[r, :, :HD], (((1,), (1,)), ((), ())), preferred_element_type=F32
        )
        j = lax.broadcasted_iota(jnp.int32, s.shape, 1)
        s = jnp.where(j < lens[r], s, NEG)
        new = fresh[r].astype(F32)
        step = lax.broadcasted_iota(jnp.int32, (QROWS, 1), 0) % STEPS
        extra = []
        for u in range(STEPS):
            dots = jnp.sum(q.astype(F32) * new[u : u + 1, :HD], axis=1, keepdims=True)
            extra.append(jnp.where(step >= u, dots, NEG))
        top = functools.reduce(jnp.maximum, extra, jnp.max(s, axis=1, keepdims=True))
        e = jnp.exp2((s - top) * (SCALE * LOG2E))
        total = jnp.sum(e, axis=1, keepdims=True)
        sums = jnp.dot(e.astype(BF16), suffix[r, :, HD:], preferred_element_type=F32)
        for u in range(STEPS):
            e = jnp.exp2((extra[u] - top) * (SCALE * LOG2E))
            total += e
            sums += e * new[u : u + 1, HD:]
        out[r] = sums / total
        lse[r] = jnp.broadcast_to(top * SCALE + jnp.log(total), (QROWS, HD))


def combine_kernel(copies, where, prompts, slots, back, local, local_lse, spread):
    held = local.shape[0]
    attn = []
    for r, (slot, rank) in enumerate(places(where[0] * held, prompts, slots, held)):
        parts, lses = [local[r]], [local_lse[r][:, :1]]
        lane = lax.broadcasted_iota(jnp.int32, (QROWS, HD), 1)
        row = lax.broadcasted_iota(jnp.int32, (QROWS, HD), 0)
        for i in range(copies):
            block = back[slot * copies + i].astype(F32)
            parts.append(jnp.where(rank == 0, block[:QROWS], block[QROWS : 2 * QROWS]))
            at = MOST * QROWS
            lse = (block[at : at + 1] + block[at + 1 : at + 2]) + block[at + 2 : at + 3]
            lse = jnp.where(lane == rank * QROWS + row, lse, 0.0)
            lses.append(jnp.sum(lse, axis=1, keepdims=True))
        top = functools.reduce(jnp.maximum, lses)
        weights = [jnp.exp(lse - top) for lse in lses]
        total = functools.reduce(jnp.add, [w * p for w, p in zip(weights, parts)])
        total = total / functools.reduce(jnp.add, weights)
        attn.append(jnp.concatenate([total[h * STEPS : (h + 1) * STEPS] for h in range(GROUP)], axis=1))
    attn = jnp.concatenate(attn, axis=0).astype(BF16)
    for i in range(spread.shape[0]):
        spread[i] = attn


def per_device(
    queries, new_kv, suffix_cache, suffix_len, prefix_cache, prompt_len, prompt_slot, sample_prompt, out_weight
):
    wide = lax.axis_size("wide")
    kvs = lax.axis_size("kv")
    held = queries.shape[0]
    ring = wide // NPROMPT
    chips = ring // CORES
    position = lax.axis_index("wide")
    x = position % ring // CORES

    def index(z, x, c):
        return (z * chips + x) * CORES + c

    planes, xs, cores = range(NPROMPT), range(chips), range(CORES)
    same_x = [[index(z, x, c) for z in planes for c in cores] for x in xs]
    along_xy = [[index(z, x, c) * kvs + y for x in xs for y in range(kvs)] for z in planes for c in cores]
    peers = NPROMPT * CORES

    def shifted(block, by):
        pairs = [(index(z, x, c), index(z, (x + by) % chips, c)) for z in planes for x in xs for c in cores]
        return lax.ppermute(block, "wide", pairs)

    where = jnp.stack([position, position // ring] + [(x - k) % chips * CORES + position % CORES for k in xs])
    prompts = sample_prompt[:, 0]

    sent, rows, cache = call(
        functools.partial(asking_kernel, CORES),
        "asking",
        [shape(peers, MOST * QROWS, HD), shape(held, QROWS, HD), shape(PSH, 2 * HD)],
        [where, prompts, prompt_slot],
        [queries, prefix_cache[:, 0, :]],
    )
    asked = lax.all_to_all(sent, "wide", 0, 0, tiled=True, axis_index_groups=same_x)
    caches = [cache] + [shifted(cache, k) for k in range(1, chips)]

    reply, weight = call(
        functools.partial(prefix_kernel, chips),
        "prefix",
        [shape(peers, MOST * QROWS + LSE_ROWS, HD), shape(*out_weight.shape)],
        [where, prompt_slot, prompt_len],
        [asked, *caches, out_weight],
        flops=4 * peers * MOST * QROWS * chips * PSH * HD,
        exps=peers * MOST * QROWS * chips * PSH,
    )
    back = lax.all_to_all(reply, "wide", 0, 0, tiled=True, axis_index_groups=same_x)
    weights = [weight] + [shifted(weight, k) for k in range(1, chips)]

    local, local_lse = call(
        local_kernel,
        "local",
        [shape(held, QROWS, HD, dtype=F32)] * 2,
        [suffix_len],
        [rows, suffix_cache[:, :, 0, :], new_kv[:, :, 0, :]],
        flops=4 * held * QROWS * suffix_cache.shape[1] * HD,
    )
    spread = call(
        functools.partial(combine_kernel, CORES),
        "combine",
        [shape(peers, held * STEPS, GROUP * HD)],
        [where, prompts, prompt_slot],
        [back, local, local_lse],
    )[0]
    spread, weights[1], weights[3] = lax.optimization_barrier((spread, weights[1], weights[3]))

    rows_in = lax.all_to_all(spread, "wide", 0, 0, tiled=True, axis_index_groups=same_x)
    rows_in = rows_in.reshape(peers * held * STEPS, GROUP * HD)
    terms = [jnp.dot(rows_in, w, preferred_element_type=F32).astype(BF16) for w in weights]
    turned = [terms[-k % chips] for k in xs]
    terms = lax.dynamic_slice_in_dim(jnp.stack(turned + turned[:-1]), (chips - x) % chips, chips)
    terms = terms.reshape(chips * NPROMPT, CORES * held * STEPS, HD)
    terms = lax.all_to_all(terms, ("wide", "kv"), 0, 0, tiled=True, axis_index_groups=along_xy)
    terms = terms.reshape(chips, kvs, CORES * held * STEPS, HD)
    mine = jnp.sum(terms.astype(F32), axis=1).astype(BF16)
    return mine.reshape(ring * held, STEPS, HD)


def solution(mesh):
    return jax.shard_map(
        per_device,
        mesh=mesh,
        in_specs=(
            P("wide", None, "kv"),
            P("wide", None, "kv", None),
            P("wide", None, "kv", None),
            P("wide"),
            P("wide", "kv", None),
            P(),
            P(),
            P(),
            P("kv", "wide"),
        ),
        out_specs=P("kv", None, "wide"),
        check_vma=False,
    )
```

```python
import functools
import math

import jax
import jax.numpy as jnp
from jax import lax
from jax.experimental import pallas as pl
from jax.experimental.pallas import tpu as pltpu
from jax.sharding import PartitionSpec as P

HD = 128
GROUP = 8
STEPS = 2
PSH = 512
NPROMPT = 8
MOST = 2
CORES = 2
QROWS = STEPS * GROUP
LSE_ROWS = 8
CHUNK = 4
NEG = -1e30
SCALE = HD ** (-0.5)
LOG2E = 1.0 / math.log(2.0)
F32 = jnp.float32
BF16 = jnp.bfloat16
VMEM = pl.BlockSpec(memory_space=pltpu.VMEM)
SMEM = pl.BlockSpec(memory_space=pltpu.SMEM)


def shape(*dims, dtype=BF16):
    return jax.ShapeDtypeStruct(dims, dtype)


def call(kernel, name, out_shape, scalars, arrays, flops=0, exps=0):
    outs = list(out_shape)
    moved = sum(math.prod(a.shape) * a.dtype.itemsize for a in list(arrays) + outs)
    return pl.pallas_call(
        kernel,
        out_shape=outs,
        in_specs=[SMEM] * len(scalars) + [VMEM] * len(arrays),
        out_specs=[VMEM] * len(outs),
        compiler_params=pltpu.CompilerParams(vmem_limit_bytes=24 * 1024 * 1024),
        cost_estimate=pl.CostEstimate(flops=flops, bytes_accessed=moved, transcendentals=exps),
        name=name,
    )(*scalars, *arrays)


def places(first, prompts, slots, held):
    mine = [prompts[first + r] for r in range(held)]
    ranks = [
        sum(((mine[e] == mine[r]).astype(jnp.int32) for e in range(r)), jnp.int32(0)) for r in range(held)
    ]
    return [(slots[mine[r]], ranks[r]) for r in range(held)]


def asking_kernel(copies, where, prompts, slots, queries, cache, sent, rows, cache_out):
    held = queries.shape[0]
    cache_out[...] = cache[...]
    sent[...] = jnp.zeros_like(sent)
    for r, (slot, rank) in enumerate(places(where[0] * held, prompts, slots, held)):
        q = queries[r].astype(F32)
        q = jnp.concatenate([q[:, h * HD : (h + 1) * HD] for h in range(GROUP)], axis=0).astype(BF16)
        rows[r] = q
        for i in range(copies):
            sent[slot * copies + i, pl.ds(pl.multiple_of(rank * QROWS, QROWS), QROWS), :] = q


def split3(x):
    hi = x.astype(BF16).astype(F32)
    mid = (x - hi).astype(BF16).astype(F32)
    return hi, mid, x - hi - mid


def prefix_kernel(segments, where, slots, lens, asked, *refs):
    blocks, weight, reply, weight_out = refs[:-3], *refs[-3:]
    weight_out[...] = weight[...]
    length = jnp.int32(0)
    for p in range(NPROMPT):
        length = jnp.where(slots[p] == where[1], lens[p], length)
    per_source = MOST * QROWS
    some = CHUNK * per_source
    for first in range(0, asked.shape[0], CHUNK):
        rows = asked[first : first + CHUNK].reshape(some, HD)
        scores = []
        for k, block in enumerate(blocks):
            s = lax.dot_general(
                rows, block[:, :HD], (((1,), (1,)), ((), ())), preferred_element_type=F32
            )
            j = lax.broadcasted_iota(jnp.int32, (1, PSH), 1)
            scores.append(jnp.where(j < length - where[2 + k] * PSH, s, NEG))
        top = functools.reduce(jnp.maximum, [jnp.max(s, axis=1, keepdims=True) for s in scores])
        floor = jnp.maximum(top, 0.1 * NEG) * (SCALE * LOG2E)
        total, part = 0.0, 0.0
        for s, block in zip(scores, blocks):
            e = jnp.exp2(s * (SCALE * LOG2E) - floor)
            total += jnp.sum(e, axis=1, keepdims=True)
            part += jnp.dot(e.astype(BF16), block[:, HD:], preferred_element_type=F32)
        safe = jnp.maximum(total, 1.0)
        part = part / safe
        lse = jnp.where(total > 0.0, top * SCALE + jnp.log(safe), NEG)
        row = lax.broadcasted_iota(jnp.int32, (some, HD), 0)
        lane = lax.broadcasted_iota(jnp.int32, (some, HD), 1)
        lse = jnp.where(row % per_source == lane, lse, 0.0).reshape(CHUNK, per_source, HD)
        lse = jnp.sum(lse, axis=1, keepdims=True)
        hi, mid, low = split3(lse)
        at = lax.broadcasted_iota(jnp.int32, (CHUNK, LSE_ROWS, HD), 1)
        pieces = jnp.where(at == 0, hi, jnp.where(at == 1, mid, jnp.where(at == 2, low, 0.0)))
        reply[first : first + CHUNK] = jnp.concatenate(
            [part.reshape(CHUNK, per_source, HD).astype(BF16), pieces.astype(BF16)], axis=1
        )


def local_kernel(lens, rows, suffix, fresh, out, lse):
    for r in range(rows.shape[0]):
        q = rows[r]
        s = lax.dot_general(
            q, suffix[r, :, :HD], (((1,), (1,)), ((), ())), preferred_element_type=F32
        )
        j = lax.broadcasted_iota(jnp.int32, s.shape, 1)
        s = jnp.where(j < lens[r], s, NEG)
        new = fresh[r].astype(F32)
        step = lax.broadcasted_iota(jnp.int32, (QROWS, 1), 0) % STEPS
        extra = []
        for u in range(STEPS):
            dots = jnp.sum(q.astype(F32) * new[u : u + 1, :HD], axis=1, keepdims=True)
            extra.append(jnp.where(step >= u, dots, NEG))
        top = functools.reduce(jnp.maximum, extra, jnp.max(s, axis=1, keepdims=True))
        e = jnp.exp2((s - top) * (SCALE * LOG2E))
        total = jnp.sum(e, axis=1, keepdims=True)
        sums = jnp.dot(e.astype(BF16), suffix[r, :, HD:], preferred_element_type=F32)
        for u in range(STEPS):
            e = jnp.exp2((extra[u] - top) * (SCALE * LOG2E))
            total += e
            sums += e * new[u : u + 1, HD:]
        out[r] = sums / total
        lse[r] = jnp.broadcast_to(top * SCALE + jnp.log(total), (QROWS, HD))


def combine_kernel(copies, where, prompts, slots, back, local, local_lse, spread):
    held = local.shape[0]
    attn = []
    for r, (slot, rank) in enumerate(places(where[0] * held, prompts, slots, held)):
        parts, lses = [local[r]], [local_lse[r][:, :1]]
        lane = lax.broadcasted_iota(jnp.int32, (QROWS, HD), 1)
        row = lax.broadcasted_iota(jnp.int32, (QROWS, HD), 0)
        for i in range(copies):
            block = back[slot * copies + i].astype(F32)
            parts.append(jnp.where(rank == 0, block[:QROWS], block[QROWS : 2 * QROWS]))
            at = MOST * QROWS
            lse = (block[at : at + 1] + block[at + 1 : at + 2]) + block[at + 2 : at + 3]
            lse = jnp.where(lane == rank * QROWS + row, lse, 0.0)
            lses.append(jnp.sum(lse, axis=1, keepdims=True))
        top = functools.reduce(jnp.maximum, lses)
        weights = [jnp.exp(lse - top) for lse in lses]
        total = functools.reduce(jnp.add, [w * p for w, p in zip(weights, parts)])
        total = total / functools.reduce(jnp.add, weights)
        attn.append(jnp.concatenate([total[h * STEPS : (h + 1) * STEPS] for h in range(GROUP)], axis=1))
    attn = jnp.concatenate(attn, axis=0).astype(BF16)
    for i in range(spread.shape[0]):
        spread[i] = attn


def per_device(
    queries, new_kv, suffix_cache, suffix_len, prefix_cache, prompt_len, prompt_slot, sample_prompt, out_weight
):
    wide = lax.axis_size("wide")
    kvs = lax.axis_size("kv")
    held = queries.shape[0]
    ring = wide // NPROMPT
    chips = ring // CORES
    position = lax.axis_index("wide")
    x = position % ring // CORES

    def index(z, x, c):
        return (z * chips + x) * CORES + c

    planes, xs, cores = range(NPROMPT), range(chips), range(CORES)
    same_x = [[index(z, x, c) for z in planes for c in cores] for x in xs]
    peers = NPROMPT * CORES

    def shifted(block, by):
        pairs = [(index(z, x, c), index(z, (x + by) % chips, c)) for z in planes for x in xs for c in cores]
        return lax.ppermute(block, "wide", pairs)

    halves, pair = chips // 2, range(2)
    equals = [[index(z, 2 * h + a, c) for z in planes for h in range(halves)] for a in pair for c in cores]
    quads = [
        [index(z, 2 * h + a, c) * kvs + y for a in pair for c in cores for y in range(kvs)]
        for z in planes
        for h in range(halves)
    ]

    def quad(block):
        beside = lax.ppermute(block, "wide", [(i, i ^ CORES) for i in range(wide)])
        other_core = [(i, i ^ 1) for i in range(wide)]
        return [block, beside, lax.ppermute(block, "wide", other_core), lax.ppermute(beside, "wide", other_core)]

    where = jnp.stack([position, position // ring] + [(x - k) % chips * CORES + position % CORES for k in xs])
    prompts = sample_prompt[:, 0]

    sent, rows, cache = call(
        functools.partial(asking_kernel, CORES),
        "asking",
        [shape(peers, MOST * QROWS, HD), shape(held, QROWS, HD), shape(PSH, 2 * HD)],
        [where, prompts, prompt_slot],
        [queries, prefix_cache[:, 0, :]],
    )
    asked = lax.all_to_all(sent, "wide", 0, 0, tiled=True, axis_index_groups=same_x)
    caches = [cache] + [shifted(cache, k) for k in range(1, chips)]

    reply, weight = call(
        functools.partial(prefix_kernel, chips),
        "prefix",
        [shape(peers, MOST * QROWS + LSE_ROWS, HD), shape(*out_weight.shape)],
        [where, prompt_slot, prompt_len],
        [asked, *caches, out_weight],
        flops=4 * peers * MOST * QROWS * chips * PSH * HD,
        exps=peers * MOST * QROWS * chips * PSH,
    )
    back = lax.all_to_all(reply, "wide", 0, 0, tiled=True, axis_index_groups=same_x)
    weights = quad(weight)

    local, local_lse = call(
        local_kernel,
        "local",
        [shape(held, QROWS, HD, dtype=F32)] * 2,
        [suffix_len],
        [rows, suffix_cache[:, :, 0, :], new_kv[:, :, 0, :]],
        flops=4 * held * QROWS * suffix_cache.shape[1] * HD,
    )
    spread = call(
        functools.partial(combine_kernel, CORES),
        "combine",
        [shape(NPROMPT * halves, held * STEPS, GROUP * HD)],
        [where, prompts, prompt_slot],
        [back, local, local_lse],
    )[0]
    spread, weights[1], weights[2] = lax.optimization_barrier((spread, weights[1], weights[2]))

    rows_in = lax.all_to_all(spread, "wide", 0, 0, tiled=True, axis_index_groups=equals)
    rows_in = rows_in.reshape(-1, GROUP * HD)
    terms = [jnp.dot(rows_in, w, preferred_element_type=F32).astype(BF16) for w in weights]
    terms = [jnp.where(x % 2 == a, terms[2 * c], terms[2 * c + 1]) for a in pair for c in cores]
    terms = [jnp.where(position % CORES == c, terms[2 * a], terms[2 * a + 1]) for a in pair for c in cores]
    terms = jnp.stack(terms).reshape(2 * CORES * NPROMPT, halves * held * STEPS, HD)
    terms = lax.all_to_all(terms, ("wide", "kv"), 0, 0, tiled=True, axis_index_groups=quads)
    terms = terms.reshape(2, CORES, kvs, halves, held * STEPS, HD)
    mine = jnp.sum(terms.astype(F32), axis=2).astype(BF16)
    return mine.transpose(2, 0, 1, 3, 4).reshape(ring * held, STEPS, HD)


def solution(mesh):
    return jax.shard_map(
        per_device,
        mesh=mesh,
        in_specs=(
            P("wide", None, "kv"),
            P("wide", None, "kv", None),
            P("wide", None, "kv", None),
            P("wide"),
            P("wide", "kv", None),
            P(),
            P(),
            P(),
            P("kv", "wide"),
        ),
        out_specs=P("kv", None, "wide"),
        check_vma=False,
    )
```

```python
import functools
import math

import jax
import jax.numpy as jnp
from jax import lax
from jax.experimental import pallas as pl
from jax.experimental.pallas import tpu as pltpu
from jax.sharding import PartitionSpec as P

HD = 128
GROUP = 8
STEPS = 2
PSH = 512
NPROMPT = 8
MOST = 2
CORES = 2
QROWS = STEPS * GROUP
LSE_ROWS = 8
CHUNK = 8
NEG = -1e30
SCALE = HD ** (-0.5)
LOG2E = 1.0 / math.log(2.0)
F32 = jnp.float32
BF16 = jnp.bfloat16
VMEM = pl.BlockSpec(memory_space=pltpu.VMEM)
SMEM = pl.BlockSpec(memory_space=pltpu.SMEM)


def shape(*dims, dtype=BF16):
    return jax.ShapeDtypeStruct(dims, dtype)


def call(kernel, name, out_shape, scalars, arrays, flops=0, exps=0):
    outs = list(out_shape)
    moved = sum(math.prod(a.shape) * a.dtype.itemsize for a in list(arrays) + outs)
    return pl.pallas_call(
        kernel,
        out_shape=outs,
        in_specs=[SMEM] * len(scalars) + [VMEM] * len(arrays),
        out_specs=[VMEM] * len(outs),
        compiler_params=pltpu.CompilerParams(vmem_limit_bytes=24 * 1024 * 1024),
        cost_estimate=pl.CostEstimate(flops=flops, bytes_accessed=moved, transcendentals=exps),
        name=name,
    )(*scalars, *arrays)


def places(first, prompts, slots, held):
    mine = [prompts[first + r] for r in range(held)]
    ranks = [
        sum(((mine[e] == mine[r]).astype(jnp.int32) for e in range(r)), jnp.int32(0)) for r in range(held)
    ]
    return [(slots[mine[r]], ranks[r]) for r in range(held)]


def asking_kernel(copies, where, prompts, slots, queries, sent, rows):
    held = queries.shape[0]
    sent[...] = jnp.zeros_like(sent)
    for r, (slot, rank) in enumerate(places(where[0] * held, prompts, slots, held)):
        q = queries[r].astype(F32)
        q = jnp.concatenate([q[:, h * HD : (h + 1) * HD] for h in range(GROUP)], axis=0).astype(BF16)
        rows[r] = q
        for i in range(copies):
            sent[slot * copies + i, pl.ds(pl.multiple_of(rank * QROWS, QROWS), QROWS), :] = q


def split3(x):
    hi = x.astype(BF16).astype(F32)
    mid = (x - hi).astype(BF16).astype(F32)
    return hi, mid, x - hi - mid


def prefix_kernel(segments, where, slots, lens, asked, *refs):
    blocks, reply = refs[:-1], refs[-1]
    length = jnp.int32(0)
    for p in range(NPROMPT):
        length = jnp.where(slots[p] == where[1], lens[p], length)
    per_source = MOST * QROWS
    some = CHUNK * per_source
    for first in range(0, asked.shape[0], CHUNK):
        rows = asked[first : first + CHUNK].reshape(some, HD)
        scores = []
        for k, block in enumerate(blocks):
            s = lax.dot_general(
                rows, block[:, :HD], (((1,), (1,)), ((), ())), preferred_element_type=F32
            )
            j = lax.broadcasted_iota(jnp.int32, (1, PSH), 1)
            scores.append(jnp.where(j < length - where[2 + k] * PSH, s, NEG))
        top = functools.reduce(jnp.maximum, [jnp.max(s, axis=1, keepdims=True) for s in scores])
        floor = jnp.maximum(top, 0.1 * NEG) * (SCALE * LOG2E)
        total, part = 0.0, 0.0
        for s, block in zip(scores, blocks):
            e = jnp.exp2(s * (SCALE * LOG2E) - floor)
            total += jnp.sum(e, axis=1, keepdims=True)
            part += jnp.dot(e.astype(BF16), block[:, HD:], preferred_element_type=F32)
        safe = jnp.maximum(total, 1.0)
        part = part / safe
        lse = jnp.where(total > 0.0, top * SCALE + jnp.log(safe), NEG)
        row = lax.broadcasted_iota(jnp.int32, (some, HD), 0)
        lane = lax.broadcasted_iota(jnp.int32, (some, HD), 1)
        lse = jnp.where(row % per_source == lane, lse, 0.0).reshape(CHUNK, per_source, HD)
        lse = jnp.sum(lse, axis=1, keepdims=True)
        hi, mid, low = split3(lse)
        at = lax.broadcasted_iota(jnp.int32, (CHUNK, LSE_ROWS, HD), 1)
        pieces = jnp.where(at == 0, hi, jnp.where(at == 1, mid, jnp.where(at == 2, low, 0.0)))
        reply[first : first + CHUNK] = jnp.concatenate(
            [part.reshape(CHUNK, per_source, HD).astype(BF16), pieces.astype(BF16)], axis=1
        )


def local_kernel(lens, rows, suffix, fresh, out, lse):
    held = rows.shape[0]
    scores, extra, news = [], [[] for _ in range(STEPS)], []
    for r in range(held):
        q = rows[r]
        s = lax.dot_general(
            q, suffix[r, :, :HD], (((1,), (1,)), ((), ())), preferred_element_type=F32
        )
        j = lax.broadcasted_iota(jnp.int32, (1, s.shape[1]), 1)
        scores.append(jnp.where(j < lens[r], s, NEG))
        news.append(fresh[r].astype(F32))
        for u in range(STEPS):
            extra[u].append(q.astype(F32) * news[r][u : u + 1, :HD])
    scores = jnp.concatenate(scores, axis=0)
    step = lax.broadcasted_iota(jnp.int32, (held * QROWS, 1), 0) % STEPS
    dots = [jnp.sum(jnp.concatenate(e, axis=0), axis=1, keepdims=True) for e in extra]
    dots = [jnp.where(step >= u, dots[u], NEG) for u in range(STEPS)]
    top = functools.reduce(jnp.maximum, dots, jnp.max(scores, axis=1, keepdims=True))
    e = jnp.exp2((scores - top) * (SCALE * LOG2E))
    late = [jnp.exp2((d - top) * (SCALE * LOG2E)) for d in dots]
    total = functools.reduce(jnp.add, late, jnp.sum(e, axis=1, keepdims=True))
    e = e.astype(BF16)
    sums = []
    for r in range(held):
        own = slice(r * QROWS, (r + 1) * QROWS)
        part = jnp.dot(e[own], suffix[r, :, HD:], preferred_element_type=F32)
        sums.append(
            functools.reduce(jnp.add, [late[u][own] * news[r][u : u + 1, HD:] for u in range(STEPS)], part)
        )
    out[...] = (jnp.concatenate(sums, axis=0) / total).reshape(out.shape)
    lse[...] = jnp.broadcast_to(top * SCALE + jnp.log(total), (held * QROWS, HD)).reshape(lse.shape)


def combine_kernel(copies, where, prompts, slots, back, local, local_lse, spread):
    held = local.shape[0]
    lane = lax.broadcasted_iota(jnp.int32, (QROWS, HD), 1)
    row = lax.broadcasted_iota(jnp.int32, (QROWS, HD), 0)
    at = MOST * QROWS
    parts, lses = [[] for _ in range(copies)], [[] for _ in range(copies)]
    for r, (slot, rank) in enumerate(places(where[0] * held, prompts, slots, held)):
        for i in range(copies):
            block = back[slot * copies + i].astype(F32)
            parts[i].append(jnp.where(rank == 0, block[:QROWS], block[QROWS:at]))
            lse = (block[at : at + 1] + block[at + 1 : at + 2]) + block[at + 2 : at + 3]
            lses[i].append(jnp.where(lane == rank * QROWS + row, lse, 0.0))
    parts = [jnp.concatenate(p, axis=0) for p in parts] + [local[...].reshape(held * QROWS, HD)]
    lses = [jnp.sum(jnp.concatenate(p, axis=0), axis=1, keepdims=True) for p in lses]
    lses.append(local_lse[...].reshape(held * QROWS, HD)[:, :1])
    top = functools.reduce(jnp.maximum, lses)
    weights = [jnp.exp(lse - top) for lse in lses]
    total = functools.reduce(jnp.add, [w * p for w, p in zip(weights, parts)])
    total = total / functools.reduce(jnp.add, weights)
    attn = [
        jnp.concatenate(
            [total[r * QROWS + h * STEPS : r * QROWS + (h + 1) * STEPS] for h in range(GROUP)], axis=1
        )
        for r in range(held)
    ]
    attn = jnp.concatenate(attn, axis=0).astype(BF16)
    for i in range(spread.shape[0]):
        spread[i] = attn


def per_device(
    queries, new_kv, suffix_cache, suffix_len, prefix_cache, prompt_len, prompt_slot, sample_prompt, out_weight
):
    wide = lax.axis_size("wide")
    kvs = lax.axis_size("kv")
    held = queries.shape[0]
    ring = wide // NPROMPT
    chips = ring // CORES
    position = lax.axis_index("wide")
    x = position % ring // CORES

    def index(z, x, c):
        return (z * chips + x) * CORES + c

    planes, xs, cores = range(NPROMPT), range(chips), range(CORES)
    same_x = [[index(z, x, c) for z in planes for c in cores] for x in xs]
    peers = NPROMPT * CORES

    def shifted(block, by):
        pairs = [(index(z, x, c), index(z, (x + by) % chips, c)) for z in planes for x in xs for c in cores]
        return lax.ppermute(block, "wide", pairs)

    halves, pair = chips // 2, range(2)
    equals = [[index(z, 2 * h + a, c) for z in planes for h in range(halves)] for a in pair for c in cores]
    quads = [
        [index(z, 2 * h + a, c) * kvs + y for a in pair for c in cores for y in range(kvs)]
        for z in planes
        for h in range(halves)
    ]

    def quad(block):
        beside = lax.ppermute(block, "wide", [(i, i ^ CORES) for i in range(wide)])
        other_core = [(i, i ^ 1) for i in range(wide)]
        return [block, beside, lax.ppermute(block, "wide", other_core), lax.ppermute(beside, "wide", other_core)]

    where = jnp.stack([position, position // ring] + [(x - k) % chips * CORES + position % CORES for k in xs])
    prompts = sample_prompt[:, 0]

    sent, rows = call(
        functools.partial(asking_kernel, CORES),
        "asking",
        [shape(peers, MOST * QROWS, HD), shape(held, QROWS, HD)],
        [where, prompts, prompt_slot],
        [queries],
    )
    asked = lax.all_to_all(sent, "wide", 0, 0, tiled=True, axis_index_groups=same_x)
    cache = prefix_cache[:, 0, :]
    caches = [cache] + [shifted(cache, k) for k in range(1, chips)]

    reply = call(
        functools.partial(prefix_kernel, chips),
        "prefix",
        [shape(peers, MOST * QROWS + LSE_ROWS, HD)],
        [where, prompt_slot, prompt_len],
        [asked, *caches],
        flops=4 * peers * MOST * QROWS * chips * PSH * HD,
        exps=peers * MOST * QROWS * chips * PSH,
    )[0]
    back = lax.all_to_all(reply, "wide", 0, 0, tiled=True, axis_index_groups=same_x)
    weights = quad(out_weight)

    local, local_lse = call(
        local_kernel,
        "local",
        [shape(held, QROWS, HD, dtype=F32)] * 2,
        [suffix_len],
        [rows, suffix_cache[:, :, 0, :], new_kv[:, :, 0, :]],
        flops=4 * held * QROWS * suffix_cache.shape[1] * HD,
    )
    spread = call(
        functools.partial(combine_kernel, CORES),
        "combine",
        [shape(NPROMPT * halves, held * STEPS, GROUP * HD)],
        [where, prompts, prompt_slot],
        [back, local, local_lse],
    )[0]
    spread, weights[3] = lax.optimization_barrier((spread, weights[3]))

    rows_in = lax.all_to_all(spread, "wide", 0, 0, tiled=True, axis_index_groups=equals)
    rows_in = rows_in.reshape(-1, GROUP * HD)
    terms = [jnp.dot(rows_in, w, preferred_element_type=F32).astype(BF16) for w in weights]
    terms = [jnp.where(x % 2 == a, terms[2 * c], terms[2 * c + 1]) for a in pair for c in cores]
    terms = [jnp.where(position % CORES == c, terms[2 * a], terms[2 * a + 1]) for a in pair for c in cores]
    terms = jnp.stack(terms).reshape(2 * CORES * NPROMPT, halves * held * STEPS, HD)
    terms = lax.all_to_all(terms, ("wide", "kv"), 0, 0, tiled=True, axis_index_groups=quads)
    terms = terms.reshape(2, CORES, kvs, halves, held * STEPS, HD)
    mine = jnp.sum(terms.astype(F32), axis=2).astype(BF16)
    return mine.transpose(2, 0, 1, 3, 4).reshape(ring * held, STEPS, HD)


def solution(mesh):
    return jax.shard_map(
        per_device,
        mesh=mesh,
        in_specs=(
            P("wide", None, "kv"),
            P("wide", None, "kv", None),
            P("wide", None, "kv", None),
            P("wide"),
            P("wide", "kv", None),
            P(),
            P(),
            P(),
            P("kv", "wide"),
        ),
        out_specs=P("kv", None, "wide"),
        check_vma=False,
    )
```

```python
import functools
import math

import jax
import jax.numpy as jnp
from jax import lax
from jax.experimental import pallas as pl
from jax.experimental.pallas import tpu as pltpu
from jax.sharding import PartitionSpec as P

HD = 128
GROUP = 8
STEPS = 2
PSH = 512
NPROMPT = 8
MOST = 2
CORES = 2
QROWS = STEPS * GROUP
LSE_ROWS = 8
CHUNK = 8
NEG = -1e30
SCALE = HD ** (-0.5)
LOG2E = 1.0 / math.log(2.0)
F32 = jnp.float32
BF16 = jnp.bfloat16
VMEM = pl.BlockSpec(memory_space=pltpu.VMEM)
SMEM = pl.BlockSpec(memory_space=pltpu.SMEM)


def shape(*dims, dtype=BF16):
    return jax.ShapeDtypeStruct(dims, dtype)


def call(kernel, name, out_shape, scalars, arrays, flops=0, exps=0):
    outs = list(out_shape)
    moved = sum(math.prod(a.shape) * a.dtype.itemsize for a in list(arrays) + outs)
    return pl.pallas_call(
        kernel,
        out_shape=outs,
        in_specs=[SMEM] * len(scalars) + [VMEM] * len(arrays),
        out_specs=[VMEM] * len(outs),
        compiler_params=pltpu.CompilerParams(vmem_limit_bytes=24 * 1024 * 1024),
        cost_estimate=pl.CostEstimate(flops=flops, bytes_accessed=moved, transcendentals=exps),
        name=name,
    )(*scalars, *arrays)


def places(first, prompts, slots, held):
    mine = [prompts[first + r] for r in range(held)]
    ranks = [
        sum(((mine[e] == mine[r]).astype(jnp.int32) for e in range(r)), jnp.int32(0)) for r in range(held)
    ]
    return [(slots[mine[r]], ranks[r]) for r in range(held)]


def asking_kernel(copies, where, prompts, slots, queries, sent, rows):
    held = queries.shape[0]
    sent[...] = jnp.zeros_like(sent)
    for r, (slot, rank) in enumerate(places(where[0] * held, prompts, slots, held)):
        q = queries[r].astype(F32)
        q = jnp.concatenate([q[:, h * HD : (h + 1) * HD] for h in range(GROUP)], axis=0).astype(BF16)
        rows[r] = q
        for i in range(copies):
            sent[slot * copies + i, pl.ds(pl.multiple_of(rank * QROWS, QROWS), QROWS), :] = q


def split3(x):
    hi = x.astype(BF16).astype(F32)
    mid = (x - hi).astype(BF16).astype(F32)
    return hi, mid, x - hi - mid


def prefix_kernel(segments, where, slots, lens, asked, *refs):
    blocks, reply = refs[:-1], refs[-1]
    length = jnp.int32(0)
    for p in range(NPROMPT):
        length = jnp.where(slots[p] == where[1], lens[p], length)
    per_source = MOST * QROWS
    some = CHUNK * per_source
    for first in range(0, asked.shape[0], CHUNK):
        rows = asked[first : first + CHUNK].reshape(some, HD)
        scores = []
        for k, block in enumerate(blocks):
            s = lax.dot_general(
                rows, block[:, :HD], (((1,), (1,)), ((), ())), preferred_element_type=F32
            )
            j = lax.broadcasted_iota(jnp.int32, (1, PSH), 1)
            scores.append(jnp.where(j < length - where[2 + k] * PSH, s, NEG))
        top = functools.reduce(jnp.maximum, [jnp.max(s, axis=1, keepdims=True) for s in scores])
        floor = jnp.maximum(top, 0.1 * NEG) * (SCALE * LOG2E)
        total, part = 0.0, 0.0
        for s, block in zip(scores, blocks):
            e = jnp.exp2(s * (SCALE * LOG2E) - floor)
            total += jnp.sum(e, axis=1, keepdims=True)
            part += jnp.dot(e.astype(BF16), block[:, HD:], preferred_element_type=F32)
        safe = jnp.maximum(total, 1.0)
        part = part / safe
        lse = jnp.where(total > 0.0, top * SCALE + jnp.log(safe), NEG)
        row = lax.broadcasted_iota(jnp.int32, (some, HD), 0)
        lane = lax.broadcasted_iota(jnp.int32, (some, HD), 1)
        lse = jnp.where(row % per_source == lane, lse, 0.0).reshape(CHUNK, per_source, HD)
        lse = jnp.sum(lse, axis=1, keepdims=True)
        hi, mid, low = split3(lse)
        at = lax.broadcasted_iota(jnp.int32, (CHUNK, LSE_ROWS, HD), 1)
        pieces = jnp.where(at == 0, hi, jnp.where(at == 1, mid, jnp.where(at == 2, low, 0.0)))
        reply[first : first + CHUNK] = jnp.concatenate(
            [part.reshape(CHUNK, per_source, HD).astype(BF16), pieces.astype(BF16)], axis=1
        )


def local_kernel(lens, rows, suffix, fresh, out, lse):
    held = rows.shape[0]
    scores, extra, news = [], [[] for _ in range(STEPS)], []
    for r in range(held):
        q = rows[r]
        s = lax.dot_general(
            q, suffix[r, :, :HD], (((1,), (1,)), ((), ())), preferred_element_type=F32
        )
        j = lax.broadcasted_iota(jnp.int32, (1, s.shape[1]), 1)
        scores.append(jnp.where(j < lens[r], s, NEG))
        news.append(fresh[r].astype(F32))
        for u in range(STEPS):
            extra[u].append(q.astype(F32) * news[r][u : u + 1, :HD])
    scores = jnp.concatenate(scores, axis=0)
    step = lax.broadcasted_iota(jnp.int32, (held * QROWS, 1), 0) % STEPS
    dots = [jnp.sum(jnp.concatenate(e, axis=0), axis=1, keepdims=True) for e in extra]
    dots = [jnp.where(step >= u, dots[u], NEG) for u in range(STEPS)]
    top = functools.reduce(jnp.maximum, dots, jnp.max(scores, axis=1, keepdims=True))
    e = jnp.exp2((scores - top) * (SCALE * LOG2E))
    late = [jnp.exp2((d - top) * (SCALE * LOG2E)) for d in dots]
    total = functools.reduce(jnp.add, late, jnp.sum(e, axis=1, keepdims=True))
    e = e.astype(BF16)
    sums = []
    for r in range(held):
        own = slice(r * QROWS, (r + 1) * QROWS)
        part = jnp.dot(e[own], suffix[r, :, HD:], preferred_element_type=F32)
        sums.append(
            functools.reduce(jnp.add, [late[u][own] * news[r][u : u + 1, HD:] for u in range(STEPS)], part)
        )
    out[...] = (jnp.concatenate(sums, axis=0) / total).reshape(out.shape)
    lse[...] = jnp.broadcast_to(top * SCALE + jnp.log(total), (held * QROWS, HD)).reshape(lse.shape)


def combine_kernel(copies, where, prompts, slots, back, local, local_lse, spread):
    held = local.shape[0]
    lane = lax.broadcasted_iota(jnp.int32, (QROWS, HD), 1)
    row = lax.broadcasted_iota(jnp.int32, (QROWS, HD), 0)
    at = MOST * QROWS
    parts, lses = [[] for _ in range(copies)], [[] for _ in range(copies)]
    for r, (slot, rank) in enumerate(places(where[0] * held, prompts, slots, held)):
        for i in range(copies):
            block = back[slot * copies + i].astype(F32)
            parts[i].append(jnp.where(rank == 0, block[:QROWS], block[QROWS:at]))
            lse = (block[at : at + 1] + block[at + 1 : at + 2]) + block[at + 2 : at + 3]
            lses[i].append(jnp.where(lane == rank * QROWS + row, lse, 0.0))
    parts = [jnp.concatenate(p, axis=0) for p in parts] + [local[...].reshape(held * QROWS, HD)]
    lses = [jnp.sum(jnp.concatenate(p, axis=0), axis=1, keepdims=True) for p in lses]
    lses.append(local_lse[...].reshape(held * QROWS, HD)[:, :1])
    top = functools.reduce(jnp.maximum, lses)
    weights = [jnp.exp(lse - top) for lse in lses]
    total = functools.reduce(jnp.add, [w * p for w, p in zip(weights, parts)])
    total = total / functools.reduce(jnp.add, weights)
    attn = [
        jnp.concatenate(
            [total[r * QROWS + h * STEPS : r * QROWS + (h + 1) * STEPS] for h in range(GROUP)], axis=1
        )
        for r in range(held)
    ]
    attn = jnp.concatenate(attn, axis=0).astype(BF16)
    for i in range(spread.shape[0]):
        spread[i] = attn


def per_device(
    queries, new_kv, suffix_cache, suffix_len, prefix_cache, prompt_len, prompt_slot, sample_prompt, out_weight
):
    wide = lax.axis_size("wide")
    kvs = lax.axis_size("kv")
    held = queries.shape[0]
    ring = wide // NPROMPT
    chips = ring // CORES
    position = lax.axis_index("wide")
    x = position % ring // CORES

    def index(z, x, c):
        return (z * chips + x) * CORES + c

    planes, xs, cores = range(NPROMPT), range(chips), range(CORES)
    same_x = [[index(z, x, c) for z in planes for c in cores] for x in xs]
    peers = NPROMPT * CORES

    def shifted(block, by):
        pairs = [(index(z, x, c), index(z, (x + by) % chips, c)) for z in planes for x in xs for c in cores]
        return lax.ppermute(block, "wide", pairs)

    halves, pair = chips // 2, range(2)
    equals = [[index(z, 2 * h + a, c) for z in planes for h in range(halves)] for a in pair for c in cores]
    quads = [
        [index(z, 2 * h + a, c) * kvs + y for a in pair for c in cores for y in range(kvs)]
        for z in planes
        for h in range(halves)
    ]

    def quad(block):
        beside = lax.ppermute(block, "wide", [(i, i ^ CORES) for i in range(wide)])
        other_core = [(i, i ^ 1) for i in range(wide)]
        return [block, beside, lax.ppermute(block, "wide", other_core), lax.ppermute(beside, "wide", other_core)]

    where = jnp.stack([position, position // ring] + [(x - k) % chips * CORES + position % CORES for k in xs])
    prompts = sample_prompt[:, 0]

    sent, rows = call(
        functools.partial(asking_kernel, CORES),
        "asking",
        [shape(peers, MOST * QROWS, HD), shape(held, QROWS, HD)],
        [where, prompts, prompt_slot],
        [queries],
    )
    asked = lax.all_to_all(sent, "wide", 0, 0, tiled=True, axis_index_groups=same_x)
    cache = prefix_cache[:, 0, :]
    caches = [cache] + [shifted(cache, k) for k in range(1, chips)]

    reply = call(
        functools.partial(prefix_kernel, chips),
        "prefix",
        [shape(peers, MOST * QROWS + LSE_ROWS, HD)],
        [where, prompt_slot, prompt_len],
        [asked, *caches],
        flops=4 * peers * MOST * QROWS * chips * PSH * HD,
        exps=peers * MOST * QROWS * chips * PSH,
    )[0]
    back = lax.all_to_all(reply, "wide", 0, 0, tiled=True, axis_index_groups=same_x)
    weights = quad(out_weight)

    local, local_lse = call(
        local_kernel,
        "local",
        [shape(held, QROWS, HD, dtype=F32)] * 2,
        [suffix_len],
        [rows, suffix_cache[:, :, 0, :], new_kv[:, :, 0, :]],
        flops=4 * held * QROWS * suffix_cache.shape[1] * HD,
    )
    spread = call(
        functools.partial(combine_kernel, CORES),
        "combine",
        [shape(NPROMPT * halves, held * STEPS, GROUP * HD)],
        [where, prompts, prompt_slot],
        [back, local, local_lse],
    )[0]
    first_chip, first_core = x % 2 == 0, position % CORES == 0
    spread, weights[3], weights[2], first_chip, first_core = lax.optimization_barrier(
        (spread, weights[3], weights[2], first_chip, first_core)
    )

    rows_in = lax.all_to_all(spread, "wide", 0, 0, tiled=True, axis_index_groups=equals)
    rows_in = rows_in.reshape(-1, GROUP * HD)
    terms = [jnp.dot(rows_in, w, preferred_element_type=F32).astype(BF16) for w in weights]
    terms = [jnp.where(first_chip, terms[2 * c + a], terms[2 * c + 1 - a]) for a in pair for c in cores]
    terms = [jnp.where(first_core, terms[2 * a + c], terms[2 * a + 1 - c]) for a in pair for c in cores]
    terms = jnp.stack(terms).reshape(2 * CORES * NPROMPT, halves * held * STEPS, HD)
    terms = lax.all_to_all(terms, ("wide", "kv"), 0, 0, tiled=True, axis_index_groups=quads)
    terms = terms.reshape(2, CORES, kvs, halves, held * STEPS, HD)
    mine = jnp.sum(terms.astype(F32), axis=2).astype(BF16)
    return mine.transpose(2, 0, 1, 3, 4).reshape(ring * held, STEPS, HD)


def solution(mesh):
    return jax.shard_map(
        per_device,
        mesh=mesh,
        in_specs=(
            P("wide", None, "kv"),
            P("wide", None, "kv", None),
            P("wide", None, "kv", None),
            P("wide"),
            P("wide", "kv", None),
            P(),
            P(),
            P(),
            P("kv", "wide"),
        ),
        out_specs=P("kv", None, "wide"),
        check_vma=False,
    )
```

```python
import functools
import math

import jax
import jax.numpy as jnp
from jax import lax
from jax.experimental import pallas as pl
from jax.experimental.pallas import tpu as pltpu
from jax.sharding import PartitionSpec as P

HD = 128
GROUP = 8
STEPS = 2
PSH = 512
NPROMPT = 8
MOST = 2
CORES = 2
QROWS = STEPS * GROUP
LSE_ROWS = 8
CHUNK = 8
NEG = -1e30
SCALE = HD ** (-0.5)
LOG2E = 1.0 / math.log(2.0)
F32 = jnp.float32
BF16 = jnp.bfloat16
VMEM = pl.BlockSpec(memory_space=pltpu.VMEM)
SMEM = pl.BlockSpec(memory_space=pltpu.SMEM)


def shape(*dims, dtype=BF16):
    return jax.ShapeDtypeStruct(dims, dtype)


def call(kernel, name, out_shape, scalars, arrays, flops=0, exps=0):
    outs = list(out_shape)
    moved = sum(math.prod(a.shape) * a.dtype.itemsize for a in list(arrays) + outs)
    return pl.pallas_call(
        kernel,
        out_shape=outs,
        in_specs=[SMEM] * len(scalars) + [VMEM] * len(arrays),
        out_specs=[VMEM] * len(outs),
        compiler_params=pltpu.CompilerParams(vmem_limit_bytes=24 * 1024 * 1024),
        cost_estimate=pl.CostEstimate(flops=flops, bytes_accessed=moved, transcendentals=exps),
        name=name,
    )(*scalars, *arrays)


def places(first, prompts, slots, held):
    mine = [prompts[first + r] for r in range(held)]
    ranks = [
        sum(((mine[e] == mine[r]).astype(jnp.int32) for e in range(r)), jnp.int32(0)) for r in range(held)
    ]
    return [(slots[mine[r]], ranks[r]) for r in range(held)]


def asking_kernel(copies, where, prompts, slots, queries, sent, rows):
    held = queries.shape[0]
    sent[...] = jnp.zeros_like(sent)
    for r, (slot, rank) in enumerate(places(where[0] * held, prompts, slots, held)):
        q = queries[r].astype(F32)
        q = jnp.concatenate([q[:, h * HD : (h + 1) * HD] for h in range(GROUP)], axis=0).astype(BF16)
        rows[r] = q
        for i in range(copies):
            sent[slot * copies + i, pl.ds(pl.multiple_of(rank * QROWS, QROWS), QROWS), :] = q


def split3(x):
    hi = x.astype(BF16).astype(F32)
    mid = (x - hi).astype(BF16).astype(F32)
    return hi, mid, x - hi - mid


def prefix_kernel(segments, where, slots, lens, asked, *refs):
    blocks, reply = refs[:-1], refs[-1]
    length = jnp.int32(0)
    for p in range(NPROMPT):
        length = jnp.where(slots[p] == where[1], lens[p], length)
    per_source = MOST * QROWS
    some = CHUNK * per_source
    for first in range(0, asked.shape[0], CHUNK):
        rows = asked[first : first + CHUNK].reshape(some, HD)
        scores = []
        for k, block in enumerate(blocks):
            s = lax.dot_general(
                rows, block[:, :HD], (((1,), (1,)), ((), ())), preferred_element_type=F32
            )
            j = lax.broadcasted_iota(jnp.int32, (1, PSH), 1)
            scores.append(jnp.where(j < length - where[2 + k] * PSH, s, NEG))
        top = functools.reduce(jnp.maximum, [jnp.max(s, axis=1, keepdims=True) for s in scores])
        floor = jnp.maximum(top, 0.1 * NEG) * (SCALE * LOG2E)
        total, part = 0.0, 0.0
        for s, block in zip(scores, blocks):
            e = jnp.exp2(s * (SCALE * LOG2E) - floor)
            total += jnp.sum(e, axis=1, keepdims=True)
            part += jnp.dot(e.astype(BF16), block[:, HD:], preferred_element_type=F32)
        safe = jnp.maximum(total, 1.0)
        part = part / safe
        lse = jnp.where(total > 0.0, top * SCALE + jnp.log(safe), NEG)
        row = lax.broadcasted_iota(jnp.int32, (some, HD), 0)
        lane = lax.broadcasted_iota(jnp.int32, (some, HD), 1)
        lse = jnp.where(row % per_source == lane, lse, 0.0).reshape(CHUNK, per_source, HD)
        lse = jnp.sum(lse, axis=1, keepdims=True)
        hi, mid, low = split3(lse)
        at = lax.broadcasted_iota(jnp.int32, (CHUNK, LSE_ROWS, HD), 1)
        pieces = jnp.where(at == 0, hi, jnp.where(at == 1, mid, jnp.where(at == 2, low, 0.0)))
        reply[first : first + CHUNK] = jnp.concatenate(
            [part.reshape(CHUNK, per_source, HD).astype(BF16), pieces.astype(BF16)], axis=1
        )


def local_kernel(lens, rows, suffix, fresh, out, lse):
    held = rows.shape[0]
    scores, extra, news = [], [[] for _ in range(STEPS)], []
    for r in range(held):
        q = rows[r]
        s = lax.dot_general(
            q, suffix[r, :, :HD], (((1,), (1,)), ((), ())), preferred_element_type=F32
        )
        j = lax.broadcasted_iota(jnp.int32, (1, s.shape[1]), 1)
        scores.append(jnp.where(j < lens[r], s, NEG))
        news.append(fresh[r].astype(F32))
        for u in range(STEPS):
            extra[u].append(q.astype(F32) * news[r][u : u + 1, :HD])
    scores = jnp.concatenate(scores, axis=0)
    step = lax.broadcasted_iota(jnp.int32, (held * QROWS, 1), 0) % STEPS
    dots = [jnp.sum(jnp.concatenate(e, axis=0), axis=1, keepdims=True) for e in extra]
    dots = [jnp.where(step >= u, dots[u], NEG) for u in range(STEPS)]
    top = functools.reduce(jnp.maximum, dots, jnp.max(scores, axis=1, keepdims=True))
    e = jnp.exp2((scores - top) * (SCALE * LOG2E))
    late = [jnp.exp2((d - top) * (SCALE * LOG2E)) for d in dots]
    total = functools.reduce(jnp.add, late, jnp.sum(e, axis=1, keepdims=True))
    e = e.astype(BF16)
    sums = []
    for r in range(held):
        own = slice(r * QROWS, (r + 1) * QROWS)
        part = jnp.dot(e[own], suffix[r, :, HD:], preferred_element_type=F32)
        sums.append(
            functools.reduce(jnp.add, [late[u][own] * news[r][u : u + 1, HD:] for u in range(STEPS)], part)
        )
    out[...] = (jnp.concatenate(sums, axis=0) / total).reshape(out.shape)
    lse[...] = jnp.broadcast_to(top * SCALE + jnp.log(total), (held * QROWS, HD)).reshape(lse.shape)


def combine_kernel(copies, where, prompts, slots, back, local, local_lse, spread):
    held = local.shape[0]
    lane = lax.broadcasted_iota(jnp.int32, (QROWS, HD), 1)
    row = lax.broadcasted_iota(jnp.int32, (QROWS, HD), 0)
    at = MOST * QROWS
    parts, lses = [[] for _ in range(copies)], [[] for _ in range(copies)]
    for r, (slot, rank) in enumerate(places(where[0] * held, prompts, slots, held)):
        for i in range(copies):
            block = back[slot * copies + i].astype(F32)
            parts[i].append(jnp.where(rank == 0, block[:QROWS], block[QROWS:at]))
            lse = (block[at : at + 1] + block[at + 1 : at + 2]) + block[at + 2 : at + 3]
            lses[i].append(jnp.where(lane == rank * QROWS + row, lse, 0.0))
    parts = [jnp.concatenate(p, axis=0) for p in parts] + [local[...].reshape(held * QROWS, HD)]
    lses = [jnp.sum(jnp.concatenate(p, axis=0), axis=1, keepdims=True) for p in lses]
    lses.append(local_lse[...].reshape(held * QROWS, HD)[:, :1])
    top = functools.reduce(jnp.maximum, lses)
    weights = [jnp.exp(lse - top) for lse in lses]
    total = functools.reduce(jnp.add, [w * p for w, p in zip(weights, parts)])
    total = total / functools.reduce(jnp.add, weights)
    attn = [
        jnp.concatenate(
            [total[r * QROWS + h * STEPS : r * QROWS + (h + 1) * STEPS] for h in range(GROUP)], axis=1
        )
        for r in range(held)
    ]
    attn = jnp.concatenate(attn, axis=0).astype(BF16)
    for i in range(spread.shape[0]):
        spread[i] = attn


def per_device(
    queries, new_kv, suffix_cache, suffix_len, prefix_cache, prompt_len, prompt_slot, sample_prompt, out_weight
):
    wide = lax.axis_size("wide")
    kvs = lax.axis_size("kv")
    held = queries.shape[0]
    ring = wide // NPROMPT
    chips = ring // CORES
    position = lax.axis_index("wide")
    x = position % ring // CORES

    def index(z, x, c):
        return (z * chips + x) * CORES + c

    planes, xs, cores = range(NPROMPT), range(chips), range(CORES)
    same_x = [[index(z, x, c) for z in planes for c in cores] for x in xs]
    peers = NPROMPT * CORES

    def shifted(block, by):
        pairs = [(index(z, x, c), index(z, (x + by) % chips, c)) for z in planes for x in xs for c in cores]
        return lax.ppermute(block, "wide", pairs)

    halves, pair = chips // 2, range(2)
    equals = [[index(z, 2 * h + a, c) for z in planes for h in range(halves)] for a in pair for c in cores]
    quads = [
        [index(z, 2 * h + a, c) * kvs + y for a in pair for c in cores for y in range(kvs)]
        for z in planes
        for h in range(halves)
    ]

    def quad(block):
        beside = lax.ppermute(block, "wide", [(i, i ^ CORES) for i in range(wide)])
        other_core = [(i, i ^ 1) for i in range(wide)]
        return [block, beside, lax.ppermute(block, "wide", other_core), lax.ppermute(beside, "wide", other_core)]

    where = jnp.stack([position, position // ring] + [(x + k) % chips * CORES + position % CORES for k in xs])
    prompts = sample_prompt[:, 0]

    sent, rows = call(
        functools.partial(asking_kernel, CORES),
        "asking",
        [shape(peers, MOST * QROWS, HD), shape(held, QROWS, HD)],
        [where, prompts, prompt_slot],
        [queries],
    )
    asked = lax.all_to_all(sent, "wide", 0, 0, tiled=True, axis_index_groups=same_x)
    cache = prefix_cache[:, 0, :]
    caches = [cache] + [shifted(cache, k) for k in reversed(range(1, chips))]

    reply = call(
        functools.partial(prefix_kernel, chips),
        "prefix",
        [shape(peers, MOST * QROWS + LSE_ROWS, HD)],
        [where, prompt_slot, prompt_len],
        [asked, *caches],
        flops=4 * peers * MOST * QROWS * chips * PSH * HD,
        exps=peers * MOST * QROWS * chips * PSH,
    )[0]
    back = lax.all_to_all(reply, "wide", 0, 0, tiled=True, axis_index_groups=same_x)
    weights = quad(out_weight)

    local, local_lse = call(
        local_kernel,
        "local",
        [shape(held, QROWS, HD, dtype=F32)] * 2,
        [suffix_len],
        [rows, suffix_cache[:, :, 0, :], new_kv[:, :, 0, :]],
        flops=4 * held * QROWS * suffix_cache.shape[1] * HD,
    )
    spread = call(
        functools.partial(combine_kernel, CORES),
        "combine",
        [shape(NPROMPT * halves, held * STEPS, GROUP * HD)],
        [where, prompts, prompt_slot],
        [back, local, local_lse],
    )[0]
    first_chip, first_core = x % 2 == 0, position % CORES == 0
    spread, weights[3], weights[2], first_chip, first_core = lax.optimization_barrier(
        (spread, weights[3], weights[2], first_chip, first_core)
    )

    rows_in = lax.all_to_all(spread, "wide", 0, 0, tiled=True, axis_index_groups=equals)
    rows_in = rows_in.reshape(-1, GROUP * HD)
    terms = [jnp.dot(rows_in, w, preferred_element_type=F32).astype(BF16) for w in weights]
    terms = [jnp.where(first_chip, terms[2 * c + a], terms[2 * c + 1 - a]) for a in pair for c in cores]
    terms = [jnp.where(first_core, terms[2 * a + c], terms[2 * a + 1 - c]) for a in pair for c in cores]
    terms = jnp.stack(terms).reshape(2 * CORES * NPROMPT, halves * held * STEPS, HD)
    terms = lax.all_to_all(terms, ("wide", "kv"), 0, 0, tiled=True, axis_index_groups=quads)
    terms = terms.reshape(2, CORES, kvs, halves, held * STEPS, HD)
    mine = jnp.sum(terms.astype(F32), axis=2).astype(BF16)
    return mine.transpose(2, 0, 1, 3, 4).reshape(ring * held, STEPS, HD)


def solution(mesh):
    return jax.shard_map(
        per_device,
        mesh=mesh,
        in_specs=(
            P("wide", None, "kv"),
            P("wide", None, "kv", None),
            P("wide", None, "kv", None),
            P("wide"),
            P("wide", "kv", None),
            P(),
            P(),
            P(),
            P("kv", "wide"),
        ),
        out_specs=P("kv", None, "wide"),
        check_vma=False,
    )
```

```python
import functools
import math

import jax
import jax.numpy as jnp
from jax import lax
from jax.experimental import pallas as pl
from jax.experimental.pallas import tpu as pltpu
from jax.sharding import PartitionSpec as P

HD = 128
GROUP = 8
STEPS = 2
PSH = 512
NPROMPT = 8
MOST = 2
CORES = 2
QROWS = STEPS * GROUP
LSE_ROWS = 8
CHUNK = 8
NEG = -1e30
SCALE = HD ** (-0.5)
LOG2E = 1.0 / math.log(2.0)
F32 = jnp.float32
BF16 = jnp.bfloat16
VMEM = pl.BlockSpec(memory_space=pltpu.VMEM)
SMEM = pl.BlockSpec(memory_space=pltpu.SMEM)


def shape(*dims, dtype=BF16):
    return jax.ShapeDtypeStruct(dims, dtype)


def call(kernel, name, out_shape, scalars, arrays, flops=0, exps=0):
    outs = list(out_shape)
    moved = sum(math.prod(a.shape) * a.dtype.itemsize for a in list(arrays) + outs)
    return pl.pallas_call(
        kernel,
        out_shape=outs,
        in_specs=[SMEM] * len(scalars) + [VMEM] * len(arrays),
        out_specs=[VMEM] * len(outs),
        compiler_params=pltpu.CompilerParams(vmem_limit_bytes=24 * 1024 * 1024),
        cost_estimate=pl.CostEstimate(flops=flops, bytes_accessed=moved, transcendentals=exps),
        name=name,
    )(*scalars, *arrays)


def places(first, prompts, slots, held):
    mine = [prompts[first + r] for r in range(held)]
    ranks = [
        sum(((mine[e] == mine[r]).astype(jnp.int32) for e in range(r)), jnp.int32(0)) for r in range(held)
    ]
    return [(slots[mine[r]], ranks[r]) for r in range(held)]


def asking_kernel(copies, where, prompts, slots, queries, sent, rows):
    held = queries.shape[0]
    sent[...] = jnp.zeros_like(sent)
    for r, (slot, rank) in enumerate(places(where[0] * held, prompts, slots, held)):
        q = queries[r].astype(F32)
        q = jnp.concatenate([q[:, h * HD : (h + 1) * HD] for h in range(GROUP)], axis=0).astype(BF16)
        rows[r] = q
        for i in range(copies):
            sent[slot * copies + i, pl.ds(pl.multiple_of(rank * QROWS, QROWS), QROWS), :] = q


def split3(x):
    hi = x.astype(BF16).astype(F32)
    mid = (x - hi).astype(BF16).astype(F32)
    return hi, mid, x - hi - mid


def prefix_kernel(segments, where, slots, lens, asked, *refs):
    blocks, reply = refs[:-1], refs[-1]
    length = jnp.int32(0)
    for p in range(NPROMPT):
        length = jnp.where(slots[p] == where[1], lens[p], length)
    per_source = MOST * QROWS
    some = CHUNK * per_source
    for first in range(0, asked.shape[0], CHUNK):
        rows = asked[first : first + CHUNK].reshape(some, HD)
        scores = []
        for k, block in enumerate(blocks):
            s = lax.dot_general(
                rows, block[:, :HD], (((1,), (1,)), ((), ())), preferred_element_type=F32
            )
            j = lax.broadcasted_iota(jnp.int32, (1, PSH), 1)
            scores.append(jnp.where(j < length - where[2 + k] * PSH, s, NEG))
        top = functools.reduce(jnp.maximum, [jnp.max(s, axis=1, keepdims=True) for s in scores])
        floor = jnp.maximum(top, 0.1 * NEG) * (SCALE * LOG2E)
        total, part = 0.0, 0.0
        for s, block in zip(scores, blocks):
            e = jnp.exp2(s * (SCALE * LOG2E) - floor)
            total += jnp.sum(e, axis=1, keepdims=True)
            part += jnp.dot(e.astype(BF16), block[:, HD:], preferred_element_type=F32)
        safe = jnp.maximum(total, 1.0)
        part = part / safe
        lse = jnp.where(total > 0.0, top * SCALE + jnp.log(safe), NEG)
        row = lax.broadcasted_iota(jnp.int32, (some, HD), 0)
        lane = lax.broadcasted_iota(jnp.int32, (some, HD), 1)
        lse = jnp.where(row % per_source == lane, lse, 0.0).reshape(CHUNK, per_source, HD)
        lse = jnp.sum(lse, axis=1, keepdims=True)
        hi, mid, low = split3(lse)
        at = lax.broadcasted_iota(jnp.int32, (CHUNK, LSE_ROWS, HD), 1)
        pieces = jnp.where(at == 0, hi, jnp.where(at == 1, mid, jnp.where(at == 2, low, 0.0)))
        reply[first : first + CHUNK] = jnp.concatenate(
            [part.reshape(CHUNK, per_source, HD).astype(BF16), pieces.astype(BF16)], axis=1
        )


def local_kernel(lens, rows, suffix, fresh, out, lse):
    held = rows.shape[0]
    scores, extra, news = [], [[] for _ in range(STEPS)], []
    for r in range(held):
        q = rows[r]
        s = lax.dot_general(
            q, suffix[r, :, :HD], (((1,), (1,)), ((), ())), preferred_element_type=F32
        )
        j = lax.broadcasted_iota(jnp.int32, (1, s.shape[1]), 1)
        scores.append(jnp.where(j < lens[r], s, NEG))
        news.append(fresh[r].astype(F32))
        for u in range(STEPS):
            extra[u].append(q.astype(F32) * news[r][u : u + 1, :HD])
    scores = jnp.concatenate(scores, axis=0)
    step = lax.broadcasted_iota(jnp.int32, (held * QROWS, 1), 0) % STEPS
    dots = [jnp.sum(jnp.concatenate(e, axis=0), axis=1, keepdims=True) for e in extra]
    dots = [jnp.where(step >= u, dots[u], NEG) for u in range(STEPS)]
    top = functools.reduce(jnp.maximum, dots, jnp.max(scores, axis=1, keepdims=True))
    e = jnp.exp2((scores - top) * (SCALE * LOG2E))
    late = [jnp.exp2((d - top) * (SCALE * LOG2E)) for d in dots]
    total = functools.reduce(jnp.add, late, jnp.sum(e, axis=1, keepdims=True))
    e = e.astype(BF16)
    sums = []
    for r in range(held):
        own = slice(r * QROWS, (r + 1) * QROWS)
        part = jnp.dot(e[own], suffix[r, :, HD:], preferred_element_type=F32)
        sums.append(
            functools.reduce(jnp.add, [late[u][own] * news[r][u : u + 1, HD:] for u in range(STEPS)], part)
        )
    out[...] = (jnp.concatenate(sums, axis=0) / total).reshape(out.shape)
    lse[...] = jnp.broadcast_to(top * SCALE + jnp.log(total), (held * QROWS, HD)).reshape(lse.shape)


def combine_kernel(copies, where, prompts, slots, back, local, local_lse, spread):
    held = local.shape[0]
    lane = lax.broadcasted_iota(jnp.int32, (QROWS, HD), 1)
    row = lax.broadcasted_iota(jnp.int32, (QROWS, HD), 0)
    at = MOST * QROWS
    parts, lses = [[] for _ in range(copies)], [[] for _ in range(copies)]
    for r, (slot, rank) in enumerate(places(where[0] * held, prompts, slots, held)):
        for i in range(copies):
            block = back[slot * copies + i].astype(F32)
            parts[i].append(jnp.where(rank == 0, block[:QROWS], block[QROWS:at]))
            lse = (block[at : at + 1] + block[at + 1 : at + 2]) + block[at + 2 : at + 3]
            lses[i].append(jnp.where(lane == rank * QROWS + row, lse, 0.0))
    parts = [jnp.concatenate(p, axis=0) for p in parts] + [local[...].reshape(held * QROWS, HD)]
    lses = [jnp.sum(jnp.concatenate(p, axis=0), axis=1, keepdims=True) for p in lses]
    lses.append(local_lse[...].reshape(held * QROWS, HD)[:, :1])
    top = functools.reduce(jnp.maximum, lses)
    weights = [jnp.exp(lse - top) for lse in lses]
    total = functools.reduce(jnp.add, [w * p for w, p in zip(weights, parts)])
    total = total / functools.reduce(jnp.add, weights)
    attn = [
        jnp.concatenate(
            [total[r * QROWS + h * STEPS : r * QROWS + (h + 1) * STEPS] for h in range(GROUP)], axis=1
        )
        for r in range(held)
    ]
    attn = jnp.concatenate(attn, axis=0).astype(BF16)
    for i in range(spread.shape[0]):
        spread[i] = attn


def per_device(
    queries, new_kv, suffix_cache, suffix_len, prefix_cache, prompt_len, prompt_slot, sample_prompt, out_weight
):
    wide = lax.axis_size("wide")
    kvs = lax.axis_size("kv")
    held = queries.shape[0]
    ring = wide // NPROMPT
    chips = ring // CORES
    position = lax.axis_index("wide")
    x = position % ring // CORES

    def index(z, x, c):
        return (z * chips + x) * CORES + c

    planes, xs, cores = range(NPROMPT), range(chips), range(CORES)
    same_x = [[index(z, x, c) for z in planes for c in cores] for x in xs]
    peers = NPROMPT * CORES

    def shifted(block, by):
        pairs = [(index(z, x, c), index(z, (x + by) % chips, c)) for z in planes for x in xs for c in cores]
        return lax.ppermute(block, "wide", pairs)

    halves, pair = chips // 2, range(2)
    equals = [[index(z, 2 * h + a, c) for z in planes for h in range(halves)] for a in pair for c in cores]
    quads = [
        [index(z, 2 * h + a, c) * kvs + y for a in pair for c in cores for y in range(kvs)]
        for z in planes
        for h in range(halves)
    ]

    def quad(block):
        beside = lax.ppermute(block, "wide", [(i, i ^ CORES) for i in range(wide)])
        other_core = [(i, i ^ 1) for i in range(wide)]
        return [block, beside, lax.ppermute(block, "wide", other_core), lax.ppermute(beside, "wide", other_core)]

    order = [0, *range(2, chips), 1]
    where = jnp.stack([position, position // ring] + [(x - k) % chips * CORES + position % CORES for k in order])
    prompts = sample_prompt[:, 0]

    sent, rows = call(
        functools.partial(asking_kernel, CORES),
        "asking",
        [shape(peers, MOST * QROWS, HD), shape(held, QROWS, HD)],
        [where, prompts, prompt_slot],
        [queries],
    )
    asked = lax.all_to_all(sent, "wide", 0, 0, tiled=True, axis_index_groups=same_x)
    cache = prefix_cache[:, 0, :]
    caches = [cache] + [shifted(cache, k) for k in order[1:]]

    reply = call(
        functools.partial(prefix_kernel, chips),
        "prefix",
        [shape(peers, MOST * QROWS + LSE_ROWS, HD)],
        [where, prompt_slot, prompt_len],
        [asked, *caches],
        flops=4 * peers * MOST * QROWS * chips * PSH * HD,
        exps=peers * MOST * QROWS * chips * PSH,
    )[0]
    back = lax.all_to_all(reply, "wide", 0, 0, tiled=True, axis_index_groups=same_x)
    weights = quad(out_weight)

    local, local_lse = call(
        local_kernel,
        "local",
        [shape(held, QROWS, HD, dtype=F32)] * 2,
        [suffix_len],
        [rows, suffix_cache[:, :, 0, :], new_kv[:, :, 0, :]],
        flops=4 * held * QROWS * suffix_cache.shape[1] * HD,
    )
    spread = call(
        functools.partial(combine_kernel, CORES),
        "combine",
        [shape(NPROMPT * halves, held * STEPS, GROUP * HD)],
        [where, prompts, prompt_slot],
        [back, local, local_lse],
    )[0]
    first_chip, first_core = x % 2 == 0, position % CORES == 0
    spread, weights[3], weights[2], first_chip, first_core = lax.optimization_barrier(
        (spread, weights[3], weights[2], first_chip, first_core)
    )

    rows_in = lax.all_to_all(spread, "wide", 0, 0, tiled=True, axis_index_groups=equals)
    rows_in = rows_in.reshape(-1, GROUP * HD)
    terms = [jnp.dot(rows_in, w, preferred_element_type=F32).astype(BF16) for w in weights]
    terms = [jnp.where(first_chip, terms[2 * c + a], terms[2 * c + 1 - a]) for a in pair for c in cores]
    terms = [jnp.where(first_core, terms[2 * a + c], terms[2 * a + 1 - c]) for a in pair for c in cores]
    terms = jnp.stack(terms).reshape(2 * CORES * NPROMPT, halves * held * STEPS, HD)
    terms = lax.all_to_all(terms, ("wide", "kv"), 0, 0, tiled=True, axis_index_groups=quads)
    terms = terms.reshape(2, CORES, kvs, halves, held * STEPS, HD)
    mine = jnp.sum(terms.astype(F32), axis=2).astype(BF16)
    return mine.transpose(2, 0, 1, 3, 4).reshape(ring * held, STEPS, HD)


def solution(mesh):
    return jax.shard_map(
        per_device,
        mesh=mesh,
        in_specs=(
            P("wide", None, "kv"),
            P("wide", None, "kv", None),
            P("wide", None, "kv", None),
            P("wide"),
            P("wide", "kv", None),
            P(),
            P(),
            P(),
            P("kv", "wide"),
        ),
        out_specs=P("kv", None, "wide"),
        check_vma=False,
    )
```
